32 devices in a mesh: grp: 4 (over z), feat: 8 (over y, x, core).
Axes of the slice: x: 2, y: 2, z: 4, core: 2. Of those that a mesh axis runs over, the one named last changes fastest.
Arguments:
- features: bfloat16 [8192, 512], P(('grp', 'feat')), may hold values from -6 to 6
- adj_tiles: bfloat16 [64, 16, 128, 128], P(('grp', 'feat')), may hold values from 0.0099487305 to 1
- src_block: int32 [64, 16], P(('grp', 'feat')), may hold values from 0 to 15, as said below
- counts: int32 [64], P(('grp', 'feat')), may hold values from 1 to 16, as said below
- w_self: bfloat16 [512, 512], replicated, may hold values from -0.25 to 0.25
- w_neigh: bfloat16 [512, 512], replicated, may hold values from -0.25 to 0.25
- multiplier: float32 [512], replicated, may hold values from 0.5 to 2
- bit_shift: int32 [512], replicated, may hold values from 0 to 2
- cotangent: bfloat16 [8192, 512], P(('grp', 'feat')), may hold values from -6 to 6
Outputs:
- output: bfloat16 [8192, 512], P(('grp', 'feat'))
- grad_features: bfloat16 [8192, 512], P(('grp', 'feat'))
- grad_self: float32 [512, 512], replicated
- grad_neigh: float32 [512, 512], replicated
The draws below stay inside these ranges and needn't reach their ends.
Inputs may be any that keep to these rules, and one draw needn't show every extreme that they name: src_block[i, k] is a block of block i's own group, held by a device at most 2 positions from block i's device in the group's cyclic order of devices (block i is held by device (i % 16) // 2 of its group, which holds 2 consecutive blocks); the distance 2 is reached in both directions in every draw. Slots k >= counts[i] take no part.
All inputs are finite; a program needn't handle non-finite values.
Results may differ from the reference program's by a relative error of at most 0.0059.
Values may be sent and summed in bfloat16 or wider, within the bound.
A program may use at most 64 MiB of HBM per device.

```python
import math
import jax
import jax.numpy as jnp
from jax import lax

F = 512
HID = 512
BLK = 128
B_DEV = 2
SLOTS = 16
SPAN = 2
BLOCKS_GRP = 16
BLOCKS = 64
NODES = 8192


def layout_draw(key):
    base = jax.random.fold_in(key, 11)
    key_a, key_b, key_c, key_d = jax.random.split(base, 4)
    spread_raw = jax.random.randint(key_a, (BLOCKS,), 0, SLOTS)
    slot_counts = 1 + spread_raw * spread_raw // SLOTS
    busiest = jax.random.randint(key_b, (), 0, BLOCKS)
    slot_counts = slot_counts.at[busiest].set(SLOTS)
    offsets = jax.random.randint(key_c, (BLOCKS, SLOTS), -SPAN, SPAN + 1)
    offsets = offsets.at[busiest, 0].set(SPAN).at[busiest, 1].set(-SPAN)
    local_pick = jax.random.randint(key_d, (BLOCKS, SLOTS), 0, B_DEV)
    group_width = BLOCKS_GRP // B_DEV
    home_dev = jnp.arange(BLOCKS, dtype=jnp.int32) % BLOCKS_GRP // B_DEV
    source_dev = (home_dev[:, None] + offsets) % group_width
    return (slot_counts.astype(jnp.int32), (source_dev * B_DEV + local_pick).astype(jnp.int32))


def draw_counts(key, part):
    return layout_draw(key)[0]


def draw_src_block(key, part):
    return layout_draw(key)[1]


def set_ends(entries, own_key, smallest, largest):
    longest = entries.shape.index(max(entries.shape))
    spots = []
    for shift in (0, 1):
        where = [jax.random.randint(jax.random.fold_in(own_key, axis), (), 0, length) for axis, length in enumerate(entries.shape)]
        where[longest] = (where[longest] + shift) % entries.shape[longest]
        spots.append(tuple(where))
    return entries.at[spots[0]].set(smallest).at[spots[1]].set(largest)


def levels(stream_key, dims, shards, low, top_value):
    gain, own = 1.0, jax.random.fold_in(stream_key, 6)
    for dim, shards_of in shards:
        heights = jnp.exp(jax.random.uniform(jax.random.fold_in(own, dim), (shards_of,), jnp.float32, low / len(shards), top_value / len(shards)))
        gain = gain * jnp.repeat(heights, dims[dim] // shards_of).reshape([-1 if axis == dim else 1 for axis in range(len(dims))])
    return gain


def scatter_about(own_key, dims, deviation, bound, cuts=(), held_as=jnp.bfloat16):
    factor_of = levels(own_key, dims, cuts, -0.22, 0.18) if cuts else 1.0
    array = jax.random.normal(own_key, dims, jnp.float32) * deviation * factor_of
    return jnp.minimum(jnp.maximum(array, -bound), bound).astype(held_as)


def setup_inputs(seed: int = 0) -> dict:
    arg_keys = jax.random.split(jax.random.key(seed), 10)
    return {
        "features": scatter_about(arg_keys[0], (NODES, F), 1.0, 6.0, ((0, 32),)),
        "adj_tiles": jnp.clip(jnp.exp(math.log(1.0) - 4.61031033 * jax.random.uniform(arg_keys[1], (BLOCKS, SLOTS, BLK, BLK), jnp.float32) ** levels(arg_keys[1], (BLOCKS, SLOTS, BLK, BLK), ((0, 32),), -0.2, 0.2)), 0.0099487305, 1.0).astype(jnp.bfloat16),
        "src_block": draw_src_block(jax.random.fold_in(arg_keys[9], 71), 0),
        "counts": draw_counts(jax.random.fold_in(arg_keys[9], 71), 0),
        "w_self": scatter_about(arg_keys[4], (F, HID), F ** -0.5, 0.25),
        "w_neigh": scatter_about(arg_keys[5], (F, HID), F ** -0.5, 0.25),
        "multiplier": jnp.clip(jnp.exp(jax.random.uniform(arg_keys[6], (HID,), jnp.float32, math.log(0.5), math.log(2.0))), 0.5, 2.0),
        "bit_shift": set_ends(jax.random.randint(arg_keys[7], (HID,), 0, 3), jax.random.fold_in(arg_keys[7], 1), 0, 2).astype(jnp.int32),
        "cotangent": scatter_about(arg_keys[8], (NODES, HID), 1.0, 6.0, ((0, 32),)),
    }


def reference(features, adj_tiles, src_block, counts, w_self, w_neigh, multiplier, bit_shift, cotangent):
    block_ids = jnp.arange(BLOCKS, dtype=jnp.int32)
    absolute = src_block + (block_ids // BLOCKS_GRP * BLOCKS_GRP)[:, None]
    live_mask = jnp.arange(SLOTS, dtype=jnp.int32)[None, :] < counts[:, None]
    masked = jnp.where(live_mask[:, :, None, None], adj_tiles, jnp.zeros_like(adj_tiles))
    degree = lax.optimization_barrier(jnp.sum(masked, axis=(1, 3), dtype=jnp.float32))
    inv_root = lax.rsqrt(degree)
    node_blocks = features.reshape(BLOCKS, BLK, F)

    def one_block(item):
        tile_set, where_src = item
        sources = node_blocks[where_src]
        return jnp.einsum('kij,kjf->if', tile_set.astype(jnp.float32), sources.astype(jnp.float32), precision=lax.Precision.HIGHEST)
    summed = lax.map(one_block, (masked, absolute))
    aggregated = (summed * inv_root[:, :, None]).astype(jnp.bfloat16).reshape(NODES, F)
    preact = jnp.dot(features, w_self, preferred_element_type=jnp.float32)
    preact = preact + jnp.dot(aggregated, w_neigh, preferred_element_type=jnp.float32)
    scale = multiplier * jnp.exp2(-bit_shift.astype(jnp.float32))
    scaled = preact * scale
    sigmoid_val = jax.nn.sigmoid(scaled)
    output = (scaled * sigmoid_val).astype(jnp.bfloat16)
    grad_pre = (cotangent.astype(jnp.float32) * sigmoid_val * (1.0 + scaled * (1.0 - sigmoid_val)) * scale).astype(jnp.bfloat16)
    grad_scale = 1.0 / math.sqrt(NODES)
    grad_self = jnp.dot(features.T, grad_pre, preferred_element_type=jnp.float32) * grad_scale
    grad_neigh = jnp.dot(aggregated.T, grad_pre, preferred_element_type=jnp.float32) * grad_scale
    own_part = jnp.dot(grad_pre, w_self.T, preferred_element_type=jnp.float32)
    back = jnp.dot(grad_pre, w_neigh.T, preferred_element_type=jnp.float32).reshape(BLOCKS, BLK, F)
    back = (back * inv_root[:, :, None]).astype(jnp.bfloat16)
    dev_count = BLOCKS // B_DEV
    tiles_dev = masked.reshape(dev_count, B_DEV, SLOTS, BLK, BLK)
    back_dev = back.reshape(dev_count, B_DEV, BLK, F)
    src_dev = src_block.reshape(dev_count, B_DEV * SLOTS)
    dev_ids = jnp.arange(dev_count, dtype=jnp.int32)

    def step(carry, item):
        dev_index, tile_set, back_rows, where_src = item
        contrib = jnp.einsum('bkij,bif->bkjf', tile_set.astype(jnp.float32), back_rows.astype(jnp.float32), precision=lax.Precision.HIGHEST).reshape(B_DEV * SLOTS, BLK, F)
        gathered = jax.ops.segment_sum(contrib, where_src, num_segments=BLOCKS_GRP)
        rounded = lax.optimization_barrier(gathered.astype(jnp.bfloat16)).astype(jnp.float32)
        base = (dev_index // (BLOCKS_GRP // B_DEV) * BLOCKS_GRP).astype(jnp.int32)
        current = lax.dynamic_slice_in_dim(carry, base, BLOCKS_GRP, 0)
        return (lax.dynamic_update_slice_in_dim(carry, current + rounded, base, 0), None)
    spread, _ = lax.scan(step, jnp.zeros((BLOCKS, BLK, F), jnp.float32), (dev_ids, tiles_dev, back_dev, src_dev))
    grad_features = (own_part + spread.reshape(NODES, F)).astype(jnp.bfloat16)
    return (output, grad_features, grad_self, grad_neigh)
```

```python
import functools
import math

import jax
import jax.numpy as jnp
from jax import lax
from jax.experimental import pallas as pl
from jax.experimental.pallas import tpu as pltpu
from jax.sharding import PartitionSpec as P

SPAN = 2
WIN = 2 * SPAN + 1
MESH = pl.DeviceIdType.MESH
LANES = 128
STRIP = 32


def dot_nn(a, b):
    return jnp.dot(a, b, preferred_element_type=jnp.float32)


def dot_tn(a, b):
    return lax.dot_general(a, b, (((0,), (0,)), ((), ())), preferred_element_type=jnp.float32)


def dot_nt(a, b):
    return lax.dot_general(a, b, (((1,), (1,)), ((), ())), preferred_element_type=jnp.float32)


def strips(rows, body, step=STRIP):
    def run(i, carry):
        body(pl.ds(pl.multiple_of(i * step, step), step))
        return carry

    lax.fori_loop(0, rows // step, run, 0)


def kernel(
    n_feat, n_grp,
    src_ref, cnt_ref, feat_ref, adj_ref, ws_ref, wn_ref, scale_ref, cot_ref,
    out_ref, gfeat_ref, grads_ref,
    pool, dense, dsum, inv, summed, preact, both, gpre,
    part_out, part_own, part_in, buf1, in2, buf2, in3, full,
    back, term_out, term_sum, term_in,
    halo_s, halo_r, term_s, term_r,
    rs1_s, rs1_r, rs2_s, rs2_r, rs3_s, rs3_r,
    ag1_s, ag1_r, ag2_s, ag2_r, ag3_s, ag3_r,
):
    n_chip = n_feat // 2
    me = lax.axis_index("feat")
    grp = lax.axis_index("grp")
    core = lax.rem(me, 2)
    chip = me // 2
    partner = me + 1 - 2 * core
    num_blocks, num_slots, block_len, _ = adj_ref.shape
    rows, width = feat_ref.shape
    ahead = lax.rem(me + 2, n_feat)
    behind = lax.rem(me + n_feat - 2, n_feat)
    chip_peers = [2 * lax.rem(chip + j, n_chip) + core for j in range(1, n_chip)]
    grp_peers = [lax.rem(grp + j, n_grp) for j in range(1, n_grp)]

    def to_feat(peer):
        return (grp, peer)

    def to_grp(peer):
        return (peer, me)

    def send(src, dst, ssem, rsem, device):
        copy = pltpu.make_async_remote_copy(
            src_ref=src, dst_ref=dst, send_sem=ssem, recv_sem=rsem, device_id=device, device_id_type=MESH
        )
        copy.start()
        return copy

    def landed(dst, rsem):
        pltpu.make_async_remote_copy(
            src_ref=dst, dst_ref=dst, send_sem=rsem, recv_sem=rsem, device_id=to_feat(partner), device_id_type=MESH
        ).wait_recv()

    sent = []

    barrier = pltpu.get_barrier_semaphore()
    partners = [to_feat(partner)] + [to_feat(p) for p in chip_peers] + [to_grp(p) for p in grp_peers]
    for device in partners:
        pl.semaphore_signal(barrier, inc=1, device_id=device, device_id_type=MESH)
    pl.semaphore_wait(barrier, len(partners))

    sent.append(send(feat_ref, pool.at[0], halo_s.at[0], halo_r.at[0], to_feat(ahead)))
    sent.append(send(feat_ref, pool.at[4], halo_s.at[1], halo_r.at[4], to_feat(behind)))
    near = 3 - 2 * core
    passed = 1 + 2 * core
    sent.append(send(feat_ref, pool.at[passed], halo_s.at[2], halo_r.at[passed], to_feat(partner)))

    dsum[...] = jnp.zeros_like(dsum)

    def build(piece, carry):
        owner = lax.rem(me + piece - SPAN + n_feat, n_feat)
        for b in range(num_blocks):
            dst_rows = slice(b * block_len, (b + 1) * block_len)
            for h in range(num_blocks):
                source = owner * num_blocks + h
                acc = jnp.zeros((block_len, block_len), jnp.float32)
                for k in range(num_slots):
                    hit = jnp.logical_and(src_ref[b, k] == source, cnt_ref[b] > k)
                    acc = acc + adj_ref[b, k].astype(jnp.float32) * jnp.where(hit, 1.0, 0.0)
                dsum[dst_rows, :] += acc
                dense[piece, dst_rows, h * block_len : (h + 1) * block_len] = acc.astype(jnp.bfloat16)
        return carry

    lax.fori_loop(0, WIN, build, 0)
    inv[...] = jnp.broadcast_to(lax.rsqrt(jnp.sum(dsum[...], axis=1, keepdims=True)), inv.shape)
    both[0] = feat_ref[...]
    preact[...] = dot_nn(feat_ref[...], ws_ref[...])
    summed[...] = dot_nn(dense[SPAN], feat_ref[...])

    landed(pool.at[near], halo_r.at[near])
    summed[...] += dot_nn(dense[near], pool[near])
    far = 4 - 4 * core
    landed(pool.at[far], halo_r.at[far])
    sent.append(send(pool.at[far], pool.at[near], halo_s.at[3], halo_r.at[near], to_feat(partner)))
    summed[...] += dot_nn(dense[far], pool[far])
    other = 4 * core
    landed(pool.at[other], halo_r.at[other])
    summed[...] += dot_nn(dense[other], pool[other])
    landed(pool.at[passed], halo_r.at[passed])
    summed[...] += dot_nn(dense[passed], pool[passed])

    def aggregate(at):
        both[1, at, :] = (summed[at, :] * inv[at, :1]).astype(jnp.bfloat16)

    strips(rows, aggregate)
    preact[...] += dot_nn(both[1], wn_ref[...])

    def activate(at):
        scale = scale_ref[...]
        scaled = preact[at, :] * scale
        gate = 1.0 / (1.0 + jnp.exp(-scaled))
        out_ref[at, :] = (scaled * gate).astype(jnp.bfloat16)
        gpre[at, :] = (
            cot_ref[at, :].astype(jnp.float32) * gate * (1.0 + scaled * (1.0 - gate)) * scale
        ).astype(jnp.bfloat16)

    strips(rows, activate)

    panels = width // LANES
    given = dot_tn(both[1 - core], gpre[...])
    for j in range(panels):
        part_out[j * width : (j + 1) * width, :] = given[:, j * LANES : (j + 1) * LANES].astype(jnp.bfloat16)
    sent.append(send(part_out, part_in, rs1_s, rs1_r, to_feat(partner)))
    kept = dot_tn(both[core], gpre[...])
    for j in range(panels):
        part_own[j * width : (j + 1) * width, :] = kept[:, j * LANES : (j + 1) * LANES]

    pulled = dot_nt(gpre[...], wn_ref[...])
    back[...] = (pulled * inv[:, :1]).astype(jnp.bfloat16)
    term_out[passed] = dot_tn(dense[passed], back[...]).astype(jnp.bfloat16)
    sent.append(send(term_out.at[passed], term_in.at[2], term_s.at[0], term_r.at[2], to_feat(partner)))

    landed(part_in, rs1_r)

    def merge1(at):
        buf1[at, :] = (part_own[at, :] + part_in[at, :].astype(jnp.float32)).astype(jnp.bfloat16)

    strips(buf1.shape[0], merge1, 128)
    c2 = buf2.shape[0]
    c3 = c2 // n_grp
    for j, peer in enumerate(chip_peers):
        at = pl.ds(pl.multiple_of((peer // 2) * c2, c2), c2)
        sent.append(send(buf1.at[at], in2.at[j], rs2_s.at[j], rs2_r.at[j], to_feat(peer)))

    term_out[other] = dot_tn(dense[other], back[...]).astype(jnp.bfloat16)
    sent.append(
        send(term_out.at[other], term_in.at[far], term_s.at[1], term_r.at[far], to_feat(lax.rem(me + other - 2 + n_feat, n_feat)))
    )
    term_sum[...] = dot_tn(dense[far], back[...])
    landed(term_in.at[2], term_r.at[2])
    term_out[far] = (term_sum[...] + term_in[2].astype(jnp.float32)).astype(jnp.bfloat16)
    sent.append(
        send(term_out.at[far], term_in.at[other], term_s.at[2], term_r.at[other], to_feat(lax.rem(me + far - 2 + n_feat, n_feat)))
    )
    term_out[near] = dot_tn(dense[near], back[...]).astype(jnp.bfloat16)
    sent.append(send(term_out.at[near], term_in.at[passed], term_s.at[3], term_r.at[passed], to_feat(partner)))
    term_sum[...] = dot_nt(gpre[...], ws_ref[...])
    term_sum[...] += dot_tn(dense[SPAN], back[...])

    for j in range(n_chip - 1):
        landed(in2.at[j], rs2_r.at[j])
    mine2 = chip * c2

    def merge2(at):
        total = buf1[pl.ds(pl.multiple_of(mine2 + at.start, 16), at.size), :].astype(jnp.float32)
        for j in range(n_chip - 1):
            total = total + in2[j, at, :].astype(jnp.float32)
        buf2[at, :] = total.astype(jnp.bfloat16)

    strips(c2, merge2, min(c2, 128))
    for j, peer in enumerate(grp_peers):
        at = pl.ds(pl.multiple_of(peer * c3, c3), c3)
        sent.append(send(buf2.at[at], in3.at[j], rs3_s.at[j], rs3_r.at[j], to_grp(peer)))
    for j in range(n_grp - 1):
        landed(in3.at[j], rs3_r.at[j])
    total = buf2[pl.ds(pl.multiple_of(grp * c3, c3), c3), :].astype(jnp.float32)
    for j in range(n_grp - 1):
        total = total + in3[j].astype(jnp.float32)
    half = buf1.shape[0]

    def piece3(owner):
        return pl.ds(pl.multiple_of(core * half + chip * c2 + owner * c3, c3), c3)

    def piece2(owner):
        return pl.ds(pl.multiple_of(core * half + owner * c2, c2), c2)

    def piece1(owner):
        return pl.ds(pl.multiple_of(owner * half, half), half)

    full[piece3(grp), :] = total.astype(jnp.bfloat16)
    for j, peer in enumerate(grp_peers):
        place = full.at[piece3(grp)]
        sent.append(send(place, place, ag3_s.at[j], ag3_r.at[j], to_grp(peer)))
    for j in range(n_grp - 1):
        landed(full.at[piece3(lax.rem(grp + n_grp - 1 - j, n_grp))], ag3_r.at[j])
    for j, peer in enumerate(chip_peers):
        place = full.at[piece2(chip)]
        sent.append(send(place, place, ag2_s.at[j], ag2_r.at[j], to_feat(peer)))

    for slot in (near, other, far):
        landed(term_in.at[slot], term_r.at[slot])

    def finish(at):
        grad = term_sum[at, :]
        for slot in (near, other, far):
            grad = grad + term_in[slot, at, :].astype(jnp.float32)
        gfeat_ref[at, :] = grad.astype(jnp.bfloat16)

    strips(rows, finish)

    for j in range(n_chip - 1):
        landed(full.at[piece2(lax.rem(chip + n_chip - 1 - j, n_chip))], ag2_r.at[j])
    place = full.at[piece1(core)]
    sent.append(send(place, place, ag1_s, ag1_r, to_feat(partner)))
    landed(full.at[piece1(1 - core)], ag1_r)
    grads_ref[...] = full[...]
    for copy in sent:
        copy.wait_send()


def local(
    n_feat, n_grp, features, adj_tiles, src_block, counts, w_self, w_neigh, multiplier, bit_shift, cotangent
):
    rows, width = features.shape
    hidden = w_self.shape[1]
    scale = (multiplier * jnp.exp2(-bit_shift.astype(jnp.float32)))[None, :]
    n_chip = n_feat // 2
    half = width * hidden // LANES
    c2 = half // n_chip
    c3 = c2 // n_grp
    bf, f32 = jnp.bfloat16, jnp.float32
    vmem = pl.BlockSpec(memory_space=pltpu.VMEM)
    smem = pl.BlockSpec(memory_space=pltpu.SMEM)
    dma = pltpu.SemaphoreType.DMA
    output, grad_features, grads = pl.pallas_call(
        functools.partial(kernel, n_feat, n_grp),
        out_shape=(
            jax.ShapeDtypeStruct((rows, hidden), bf),
            jax.ShapeDtypeStruct((rows, width), bf),
            jax.ShapeDtypeStruct((2 * half, LANES), bf),
        ),
        in_specs=[smem, smem] + [vmem] * 6,
        out_specs=(vmem, vmem, vmem),
        scratch_shapes=[
            pltpu.VMEM((WIN, rows, width), bf),
            pltpu.VMEM((WIN, rows, rows), bf),
            pltpu.VMEM((rows, adj_tiles.shape[3]), f32),
            pltpu.VMEM((rows, LANES), f32),
            pltpu.VMEM((rows, width), f32),
            pltpu.VMEM((rows, hidden), f32),
            pltpu.VMEM((2, rows, width), bf),
            pltpu.VMEM((rows, hidden), bf),
            pltpu.VMEM((half, LANES), bf),
            pltpu.VMEM((half, LANES), f32),
            pltpu.VMEM((half, LANES), bf),
            pltpu.VMEM((half, LANES), bf),
            pltpu.VMEM((n_chip - 1, c2, LANES), bf),
            pltpu.VMEM((c2, LANES), bf),
            pltpu.VMEM((n_grp - 1, c3, LANES), bf),
            pltpu.VMEM((2 * half, LANES), bf),
            pltpu.VMEM((rows, width), bf),
            pltpu.VMEM((WIN, rows, width), bf),
            pltpu.VMEM((rows, width), f32),
            pltpu.VMEM((WIN, rows, width), bf),
            dma((4,)), dma((WIN,)), dma((4,)), dma((WIN,)),
            dma, dma, dma((n_chip - 1,)), dma((n_chip - 1,)), dma((n_grp - 1,)), dma((n_grp - 1,)),
            dma, dma, dma((n_chip - 1,)), dma((n_chip - 1,)), dma((n_grp - 1,)), dma((n_grp - 1,)),
        ],
        compiler_params=pltpu.CompilerParams(
            collective_id=0, has_side_effects=True, vmem_limit_bytes=48 * 1024 * 1024
        ),
    )(src_block, counts, features, adj_tiles, w_self, w_neigh, scale, cotangent)
    grad_scale = 1.0 / math.sqrt(rows * n_grp * n_feat)
    grads = grads.reshape(2, hidden // LANES, width, LANES).transpose(0, 2, 1, 3).reshape(2, width, hidden)
    return (output, grad_features, grads[0].astype(f32) * grad_scale, grads[1].astype(f32) * grad_scale)


def solution(mesh):
    return jax.shard_map(
        functools.partial(local, mesh.shape["feat"], mesh.shape["grp"]),
        mesh=mesh,
        in_specs=(
            P(("grp", "feat"), None),
            P(("grp", "feat"), None, None, None),
            P(("grp", "feat"), None),
            P(("grp", "feat")),
            P(),
            P(),
            P(),
            P(),
            P(("grp", "feat"), None),
        ),
        out_specs=(P(("grp", "feat"), None), P(("grp", "feat"), None), P(), P()),
        check_vma=False,
    )
```

```python
import functools
import math

import jax
import jax.numpy as jnp
from jax import lax
from jax.experimental import pallas as pl
from jax.experimental.pallas import tpu as pltpu
from jax.sharding import PartitionSpec as P

SPAN = 2
WIN = 2 * SPAN + 1
MESH = pl.DeviceIdType.MESH
STRIP = 32
CHUNKS = 4
SPARE = 1
SPLIT = 3


def dot_nn(a, b):
    return jnp.dot(a, b, preferred_element_type=jnp.float32)


def dot_tn(a, b):
    return lax.dot_general(a, b, (((0,), (0,)), ((), ())), preferred_element_type=jnp.float32)


def dot_nt(a, b):
    return lax.dot_general(a, b, (((1,), (1,)), ((), ())), preferred_element_type=jnp.float32)


def strips(rows, body, step=STRIP):
    def run(i, carry):
        body(pl.ds(pl.multiple_of(i * step, step), step))
        return carry

    lax.fori_loop(0, rows // step, run, 0)


def kernel(
    n_feat, n_grp, fine,
    src_ref, cnt_ref, feat_hbm, adj_hbm, ws_hbm, wn_hbm, mult_hbm, shift_hbm, cot_hbm,
    out_hbm, gfeat_hbm, grads_hbm,
    out_ref, gfeat_ref,
    adj_ref, ws_ref, wn_ref, mult_ref, shift_ref, cot_ref,
    pool, dense, dsum, inv, summed, preact, both, gpre,
    part_out, part_own, part_in, buf1, in2, buf2, in3, full,
    back, term_out, term_sum, own_grad, term_in,
    load_s, store_s, halo_s, halo_r, term_s, term_r,
    rs1_s, rs1_r, rs2_s, rs2_r, rs3_s, rs3_r,
    ag1_s, ag1_r, ag2_s, ag2_r, ag3_s, ag3_r,
):
    n_chip = n_feat // 2
    square = n_chip == 4
    me = lax.axis_index("feat")
    grp = lax.axis_index("grp")
    core = lax.rem(me, 2)
    chip = me // 2
    odd = lax.rem(chip, 2)
    partner = me + 1 - 2 * core
    num_blocks, num_slots, block_len, _ = adj_ref.shape
    rows, width = feat_hbm.shape
    lanes = buf1.shape[1]
    ahead = lax.rem(me + 2, n_feat)
    behind = lax.rem(me + n_feat - 2, n_feat)
    chip_peers = [2 * lax.rem(chip + j, n_chip) + core for j in range(1, n_chip)]
    grp_peers = [lax.rem(grp + j, n_grp) for j in range(1, n_grp)]
    x_slot = 4 - 4 * odd
    y_slot = 4 * odd
    x_peer = 2 * (chip + 1 - 2 * odd) + core
    y_peer = 2 * lax.rem(chip + 2, n_chip) + core

    def to_feat(peer):
        return (grp, peer)

    def to_grp(peer):
        return (peer, me)

    sent = []

    def send(src, dst, ssem, rsem, device):
        copy = pltpu.make_async_remote_copy(
            src_ref=src, dst_ref=dst, send_sem=ssem, recv_sem=rsem, device_id=device, device_id_type=MESH
        )
        copy.start()
        sent.append(copy)

    def landed(dst, rsem):
        pltpu.make_async_remote_copy(
            src_ref=dst, dst_ref=dst, send_sem=rsem, recv_sem=rsem, device_id=to_feat(partner), device_id_type=MESH
        ).wait_recv()

    loads = [
        pltpu.make_async_copy(src, dst, load_s.at[i])
        for i, (src, dst) in enumerate(
            (
                (adj_hbm, adj_ref), (feat_hbm, both.at[0]), (ws_hbm, ws_ref), (wn_hbm, wn_ref),
                (mult_hbm, mult_ref), (shift_hbm, shift_ref), (cot_hbm, cot_ref),
            )
        )
    ]
    for load in loads:
        load.start()

    barrier = pltpu.get_barrier_semaphore()
    partners = [to_feat(partner)] + [to_feat(p) for p in chip_peers] + [to_grp(p) for p in grp_peers]
    for device in partners:
        pl.semaphore_signal(barrier, inc=1, device_id=device, device_id_type=MESH)
    pl.semaphore_wait(barrier, len(partners))

    near = 3 - 2 * core
    passed = 1 + 2 * core
    far = 4 - 4 * core
    other = 4 * core
    step = rows // CHUNKS
    chunks = [pl.ds(c * step, step) for c in range(CHUNKS)]
    if square:
        for c, at in enumerate(chunks):
            send(feat_hbm.at[at], pool.at[y_slot, at], halo_s.at[0, c], halo_r.at[y_slot, c], to_feat(x_peer))
    else:
        for c, at in enumerate(chunks):
            send(feat_hbm.at[at], pool.at[0, at], halo_s.at[0, c], halo_r.at[0, c], to_feat(ahead))
            send(feat_hbm.at[at], pool.at[4, at], halo_s.at[1, c], halo_r.at[4, c], to_feat(behind))
    send(feat_hbm, pool.at[passed], halo_s.at[2, 0], halo_r.at[passed, 0], to_feat(partner))

    dsum[...] = jnp.zeros_like(dsum)
    loads[0].wait()

    def build(piece, carry):
        owner = lax.rem(me + piece - SPAN + n_feat, n_feat)
        for b in range(num_blocks):
            dst_rows = slice(b * block_len, (b + 1) * block_len)
            for h in range(num_blocks):
                source = owner * num_blocks + h
                acc = jnp.zeros((block_len, block_len), jnp.float32)
                for k in range(num_slots):
                    hit = jnp.logical_and(src_ref[b, k] == source, cnt_ref[b] > k)
                    acc = acc + adj_ref[b, k].astype(jnp.float32) * jnp.where(hit, 1.0, 0.0)
                dsum[dst_rows, :] += acc
                dense[piece, dst_rows, h * block_len : (h + 1) * block_len] = acc.astype(jnp.bfloat16)
        return carry

    def relay():
        for c, at in enumerate(chunks):
            landed(pool.at[x_slot, at], halo_r.at[x_slot, c])
            if square:
                send(pool.at[x_slot, at], pool.at[y_slot, at], halo_s.at[1, c], halo_r.at[y_slot, c], to_feat(y_peer))

    lax.fori_loop(0, SPLIT, build, 0)
    relay()
    lax.fori_loop(SPLIT, WIN, build, 0)
    inv[...] = jnp.broadcast_to(lax.rsqrt(jnp.sum(dsum[...], axis=1, keepdims=True)), inv.shape)
    loads[1].wait()
    loads[2].wait()
    preact[...] = dot_nn(both[0], ws_ref[...])
    summed[...] = dot_nn(dense[SPAN], both[0])
    landed(pool.at[near], halo_r.at[near, 0])
    summed[...] += dot_nn(dense[near], pool[near])
    summed[...] += dot_nn(dense[x_slot], pool[x_slot])
    for c, at in enumerate(chunks):
        landed(pool.at[y_slot, at], halo_r.at[y_slot, c])
        send(pool.at[far, at], pool.at[near, at], halo_s.at[3, c], halo_r.at[near, SPARE + c], to_feat(partner))
    summed[...] += dot_nn(dense[y_slot], pool[y_slot])
    for load in loads[3:]:
        load.wait()
    for c, at in enumerate(chunks):
        landed(pool.at[passed, at], halo_r.at[passed, SPARE + c])
    summed[...] += dot_nn(dense[passed], pool[passed])

    def aggregate(at):
        both[1, at, :] = (summed[at, :] * inv[at, :1]).astype(jnp.bfloat16)

    strips(rows, aggregate)
    preact[...] += dot_nn(both[1], wn_ref[...])
    mult_ref[...] = mult_ref[...] * jnp.exp2(-shift_ref[...].astype(jnp.float32))

    def activate(at):
        scale = mult_ref[...]
        scaled = preact[at, :] * scale
        gate = 1.0 / (1.0 + jnp.exp(-scaled))
        out_ref[at, :] = (scaled * gate).astype(jnp.bfloat16)
        gpre[at, :] = (
            cot_ref[at, :].astype(jnp.float32) * gate * (1.0 + scaled * (1.0 - gate)) * scale
        ).astype(jnp.bfloat16)

    strips(rows, activate)
    stores = []

    def store(src, dst):
        copy = pltpu.make_async_copy(src, dst, store_s.at[len(stores)])
        copy.start()
        stores.append(copy)

    store(out_ref, out_hbm)

    half = buf1.shape[0]
    c2 = buf2.shape[0]
    c3 = c2 // n_grp
    panels = gpre.shape[1] // lanes
    given = dot_tn(both[1 - core], gpre[...])
    for j in range(panels):
        part_out[j * width : (j + 1) * width, :] = given[:, j * lanes : (j + 1) * lanes].astype(jnp.bfloat16)
    order = [lax.rem(chip + j, n_chip) for j in range(1, n_chip + 1)]
    spans = [pl.ds(pl.multiple_of(p * c2, c2), c2) for p in order]
    for j, at in enumerate(spans):
        send(part_out.at[at], part_in.at[at], rs1_s.at[j], rs1_r.at[order[j]], to_feat(partner))
    kept = dot_tn(both[core], gpre[...])
    for j in range(panels):
        part_own[j * width : (j + 1) * width, :] = kept[:, j * lanes : (j + 1) * lanes]

    pulled = dot_nt(gpre[...], wn_ref[...])
    back[...] = (pulled * inv[:, :1]).astype(jnp.bfloat16)
    term_out[passed] = dot_tn(dense[passed], back[...]).astype(jnp.bfloat16)
    send(term_out.at[passed], term_in.at[2], term_s.at[0, 0], term_r.at[2, 0], to_feat(partner))

    for j, at in enumerate(spans):
        landed(part_in.at[at], rs1_r.at[order[j]])
        buf1[at, :] = (part_own[at, :] + part_in[at, :].astype(jnp.float32)).astype(jnp.bfloat16)
    if fine:
        owners = [lax.rem(grp + 1 + q, n_grp) for q in range(n_grp)]
        cuts = [(pl.multiple_of(o * c3, c3), c3) for o in owners]
    else:
        cuts = [(0, c2)]
    for q, (first, size) in enumerate(cuts):
        for j, peer in enumerate(chip_peers):
            src = buf1.at[pl.ds(pl.multiple_of((peer // 2) * c2 + first, 16), size)]
            send(src, in2.at[j, pl.ds(first, size)], rs2_s.at[j, q], rs2_r.at[j, q], to_feat(peer))

    term_sum[0] = dot_tn(dense[x_slot], back[...])
    term_sum[1] = dot_tn(dense[y_slot], back[...])
    landed(term_in.at[2], term_r.at[2, 0])
    through = lax.rem(core + chip, 2)
    term_sum[through] += term_in[2].astype(jnp.float32)
    tstep = rows // 2
    halves = [pl.ds(c * tstep, tstep) for c in range(2)]
    for c, at in enumerate(halves):
        term_out[y_slot, at, :] = term_sum[1, at, :].astype(jnp.bfloat16)
        if square:
            send(term_out.at[y_slot, at], term_in.at[1, at], term_s.at[1, c], term_r.at[1, c], to_feat(y_peer))
        else:
            target = lax.rem(me + y_slot - 2 + n_feat, n_feat)
            send(term_out.at[y_slot, at], term_in.at[odd, at], term_s.at[1, c], term_r.at[odd, c], to_feat(target))
    term_out[near] = dot_tn(dense[near], back[...]).astype(jnp.bfloat16)
    send(term_out.at[near], term_in.at[3], term_s.at[3, 0], term_r.at[3, 0], to_feat(partner))
    own_grad[...] = dot_nt(gpre[...], ws_ref[...])
    own_grad[...] += dot_tn(dense[SPAN], back[...])

    def send_terms():
        for c, at in enumerate(halves):
            value = term_sum[0, at, :]
            if square:
                landed(term_in.at[1, at], term_r.at[1, c])
                value = value + term_in[1, at, :].astype(jnp.float32)
            term_out[x_slot, at, :] = value.astype(jnp.bfloat16)
            if square:
                send(term_out.at[x_slot, at], term_in.at[0, at], term_s.at[2, c], term_r.at[0, c], to_feat(x_peer))
            else:
                target = lax.rem(me + x_slot - 2 + n_feat, n_feat)
                place = 1 - odd
                send(term_out.at[x_slot, at], term_in.at[place, at], term_s.at[2, c], term_r.at[place, c], to_feat(target))

    if not fine:
        send_terms()

    for q, (first, size) in enumerate(cuts):
        at = pl.ds(first, size)
        total = buf1[pl.ds(pl.multiple_of(chip * c2 + first, 16), size), :].astype(jnp.float32)
        for j in range(n_chip - 1):
            landed(in2.at[j, at], rs2_r.at[j, q])
            total = total + in2[j, at, :].astype(jnp.float32)
        buf2[at, :] = total.astype(jnp.bfloat16)
        if fine and q < n_grp - 1:
            send(buf2.at[at], in3.at[q], rs3_s.at[q], rs3_r.at[q], to_grp(grp_peers[q]))
    if fine:
        send_terms()
    else:
        for j, peer in enumerate(grp_peers):
            at = pl.ds(pl.multiple_of(peer * c3, c3), c3)
            send(buf2.at[at], in3.at[j], rs3_s.at[j], rs3_r.at[j], to_grp(peer))
    total = buf2[pl.ds(pl.multiple_of(grp * c3, c3), c3), :].astype(jnp.float32)
    for j in range(n_grp - 1):
        landed(in3.at[j], rs3_r.at[j])
        total = total + in3[j].astype(jnp.float32)

    def piece3(owner):
        return full.at[pl.ds(pl.multiple_of(core * half + chip * c2 + owner * c3, c3), c3)]

    def piece2(side, owner):
        return full.at[pl.ds(pl.multiple_of(side * half + owner * c2, c2), c2)]

    def spread_piece(owner, q):
        for j, peer in enumerate(chip_peers):
            send(piece3(owner), piece3(owner), ag2_s.at[j, q], ag2_r.at[j, q], to_feat(peer))

    piece3(grp)[...] = total.astype(jnp.bfloat16)
    for j, peer in enumerate(grp_peers):
        send(piece3(grp), piece3(grp), ag3_s.at[j], ag3_r.at[j], to_grp(peer))
    if fine:
        spread_piece(grp, 0)
    for j in range(n_grp - 1):
        owner = lax.rem(grp + n_grp - 1 - j, n_grp)
        landed(piece3(owner), ag3_r.at[j])
        if fine:
            spread_piece(owner, j + 1)
    if not fine:
        for j, peer in enumerate(chip_peers):
            send(piece2(core, chip), piece2(core, chip), ag2_s.at[j, 0], ag2_r.at[j, 0], to_feat(peer))
    send(piece2(core, chip), piece2(core, chip), ag1_s.at[0], ag1_r.at[0], to_feat(partner))

    arrivals = (0, 3) if square else (0, 1, 3)
    for slot in arrivals:
        if slot == 3:
            landed(term_in.at[3], term_r.at[3, 0])
        else:
            for c, at in enumerate(halves):
                landed(term_in.at[slot, at], term_r.at[slot, c])

    def finish(at):
        grad = own_grad[at, :]
        for slot in arrivals:
            grad = grad + term_in[slot, at, :].astype(jnp.float32)
        gfeat_ref[at, :] = grad.astype(jnp.bfloat16)

    strips(rows, finish)
    store(gfeat_ref, gfeat_hbm)

    for j in range(n_chip - 1):
        owner = lax.rem(chip + n_chip - 1 - j, n_chip)
        for q in range(len(cuts)):
            if fine:
                piece = full.at[
                    pl.ds(pl.multiple_of(core * half + owner * c2 + lax.rem(grp + n_grp - q, n_grp) * c3, c3), c3)
                ]
            else:
                piece = piece2(core, owner)
            landed(piece, ag2_r.at[j, q])
        send(piece2(core, owner), piece2(core, owner), ag1_s.at[j + 1], ag1_r.at[j + 1], to_feat(partner))
    own_half = pl.ds(pl.multiple_of(core * half, half), half)
    store(full.at[own_half], grads_hbm.at[own_half])
    for j in range(n_chip):
        owner = lax.rem(chip + n_chip - j, n_chip)
        landed(piece2(1 - core, owner), ag1_r.at[j])
    its_half = pl.ds(pl.multiple_of((1 - core) * half, half), half)
    store(full.at[its_half], grads_hbm.at[its_half])
    for copy in sent:
        copy.wait_send()
    for copy in stores:
        copy.wait()


def local(
    n_feat, n_grp, features, adj_tiles, src_block, counts, w_self, w_neigh, multiplier, bit_shift, cotangent
):
    rows, width = features.shape
    hidden = w_self.shape[1]
    n_chip = n_feat // 2
    lanes = hidden if width % (16 * n_chip * n_grp) == 0 else 128
    fine = n_chip * n_grp <= 16
    half = width * hidden // lanes
    c2 = half // n_chip
    c3 = c2 // n_grp
    bf, f32 = jnp.bfloat16, jnp.float32
    smem = pl.BlockSpec(memory_space=pltpu.SMEM)
    hbm = pl.BlockSpec(memory_space=pltpu.HBM)
    dma = pltpu.SemaphoreType.DMA
    cuts = n_grp if fine else 1
    output, grad_features, grads = pl.pallas_call(
        functools.partial(kernel, n_feat, n_grp, fine),
        out_shape=(
            jax.ShapeDtypeStruct((rows, hidden), bf),
            jax.ShapeDtypeStruct((rows, width), bf),
            jax.ShapeDtypeStruct((2 * half, lanes), bf),
        ),
        in_specs=[smem, smem] + [hbm] * 7,
        out_specs=(hbm, hbm, hbm),
        scratch_shapes=[
            pltpu.VMEM((rows, hidden), bf),
            pltpu.VMEM((rows, width), bf),
            pltpu.VMEM(adj_tiles.shape, bf),
            pltpu.VMEM(w_self.shape, bf),
            pltpu.VMEM(w_neigh.shape, bf),
            pltpu.VMEM((1, hidden), f32),
            pltpu.VMEM((1, hidden), jnp.int32),
            pltpu.VMEM((rows, hidden), bf),
            pltpu.VMEM((WIN, rows, width), bf),
            pltpu.VMEM((WIN, rows, rows), bf),
            pltpu.VMEM((rows, adj_tiles.shape[3]), f32),
            pltpu.VMEM((rows, 128), f32),
            pltpu.VMEM((rows, width), f32),
            pltpu.VMEM((rows, hidden), f32),
            pltpu.VMEM((2, rows, width), bf),
            pltpu.VMEM((rows, hidden), bf),
            pltpu.VMEM((half, lanes), bf),
            pltpu.VMEM((half, lanes), f32),
            pltpu.VMEM((half, lanes), bf),
            pltpu.VMEM((half, lanes), bf),
            pltpu.VMEM((n_chip - 1, c2, lanes), bf),
            pltpu.VMEM((c2, lanes), bf),
            pltpu.VMEM((n_grp - 1, c3, lanes), bf),
            pltpu.VMEM((2 * half, lanes), bf),
            pltpu.VMEM((rows, width), bf),
            pltpu.VMEM((WIN, rows, width), bf),
            pltpu.VMEM((2, rows, width), f32),
            pltpu.VMEM((rows, width), f32),
            pltpu.VMEM((4, rows, width), bf),
            dma((7,)), dma((4,)), dma((4, CHUNKS)), dma((WIN, SPARE + CHUNKS)), dma((4, 2)), dma((4, 2)),
            dma((n_chip,)), dma((n_chip,)), dma((n_chip - 1, cuts)), dma((n_chip - 1, cuts)),
            dma((n_grp - 1,)), dma((n_grp - 1,)),
            dma((n_chip,)), dma((n_chip,)), dma((n_chip - 1, cuts)), dma((n_chip - 1, cuts)),
            dma((n_grp - 1,)), dma((n_grp - 1,)),
        ],
        compiler_params=pltpu.CompilerParams(
            collective_id=0, has_side_effects=True, vmem_limit_bytes=62 * 1024 * 1024
        ),
    )(
        src_block, counts, features, adj_tiles, w_self, w_neigh,
        multiplier.reshape(1, hidden), bit_shift.reshape(1, hidden), cotangent,
    )
    grad_scale = 1.0 / math.sqrt(rows * n_grp * n_feat)
    if lanes != hidden:
        grads = grads.reshape(2, hidden // lanes, width, lanes).transpose(0, 2, 1, 3).reshape(2 * width, hidden)
    return (
        output,
        grad_features,
        grads[:width].astype(f32) * grad_scale,
        grads[width:].astype(f32) * grad_scale,
    )


def solution(mesh):
    return jax.shard_map(
        functools.partial(local, mesh.shape["feat"], mesh.shape["grp"]),
        mesh=mesh,
        in_specs=(
            P(("grp", "feat"), None),
            P(("grp", "feat"), None, None, None),
            P(("grp", "feat"), None),
            P(("grp", "feat")),
            P(),
            P(),
            P(),
            P(),
            P(("grp", "feat"), None),
        ),
        out_specs=(P(("grp", "feat"), None), P(("grp", "feat"), None), P(), P()),
        check_vma=False,
    )
```

```python
import functools
import math

import jax
import jax.numpy as jnp
from jax import lax
from jax.experimental import pallas as pl
from jax.experimental.pallas import tpu as pltpu
from jax.sharding import PartitionSpec as P

SPAN = 2
WIN = 2 * SPAN + 1
MESH = pl.DeviceIdType.MESH
STRIP = 32
CHUNKS = 8
SPLIT = 3


def dot_nn(a, b):
    return jnp.dot(a, b, preferred_element_type=jnp.float32)


def dot_tn(a, b):
    return lax.dot_general(a, b, (((0,), (0,)), ((), ())), preferred_element_type=jnp.float32)


def dot_nt(a, b):
    return lax.dot_general(a, b, (((1,), (1,)), ((), ())), preferred_element_type=jnp.float32)


def strips(rows, body, step=STRIP):
    def run(i, carry):
        body(pl.ds(pl.multiple_of(i * step, step), step))
        return carry

    lax.fori_loop(0, rows // step, run, 0)


def kernel(
    n_feat, n_grp, fine,
    src_ref, cnt_ref, feat_hbm, adj_hbm, ws_hbm, wn_hbm, mult_hbm, shift_hbm, cot_hbm,
    out_hbm, gfeat_hbm, grads_hbm,
    out_ref, gfeat_ref,
    adj_ref, ws_ref, wn_ref, mult_ref, shift_ref, cot_ref,
    pool, dense, dsum, inv, summed, preact, both, gpre,
    buf1, in2, buf2, in3, full,
    back, term_out, term_sum, own_grad, term_in,
    load_s, store_s, halo_s, halo_r, term_s, term_r,
    pair_s, pair_r, rs2_s, rs2_r, rs3_s, rs3_r,
    ag1_s, ag1_r, ag2_s, ag2_r, ag3_s, ag3_r,
):
    n_chip = n_feat // 2
    square = n_chip == 4
    me = lax.axis_index("feat")
    grp = lax.axis_index("grp")
    core = lax.rem(me, 2)
    chip = me // 2
    odd = lax.rem(chip, 2)
    partner = me + 1 - 2 * core
    num_blocks, num_slots, block_len, _ = adj_ref.shape
    rows, width = feat_hbm.shape
    lanes = buf1.shape[1]
    ahead = lax.rem(me + 2, n_feat)
    behind = lax.rem(me + n_feat - 2, n_feat)
    chip_peers = [2 * lax.rem(chip + j, n_chip) + core for j in range(1, n_chip)]
    grp_peers = [lax.rem(grp + j, n_grp) for j in range(1, n_grp)]
    x_slot = 4 - 4 * odd
    y_slot = 4 * odd
    x_peer = 2 * (chip + 1 - 2 * odd) + core
    y_peer = 2 * lax.rem(chip + 2, n_chip) + core

    def to_feat(peer):
        return (grp, peer)

    def to_grp(peer):
        return (peer, me)

    sent = []

    def send(src, dst, ssem, rsem, device):
        copy = pltpu.make_async_remote_copy(
            src_ref=src, dst_ref=dst, send_sem=ssem, recv_sem=rsem, device_id=device, device_id_type=MESH
        )
        copy.start()
        sent.append(copy)

    def landed(dst, rsem):
        pltpu.make_async_remote_copy(
            src_ref=dst, dst_ref=dst, send_sem=rsem, recv_sem=rsem, device_id=to_feat(partner), device_id_type=MESH
        ).wait_recv()

    loads = [
        pltpu.make_async_copy(src, dst, load_s.at[i])
        for i, (src, dst) in enumerate(
            (
                (adj_hbm, adj_ref), (feat_hbm, both.at[0]), (ws_hbm, ws_ref), (wn_hbm, wn_ref),
                (mult_hbm, mult_ref), (shift_hbm, shift_ref), (cot_hbm, cot_ref),
            )
        )
    ]
    for load in loads:
        load.start()

    barrier = pltpu.get_barrier_semaphore()
    partners = [to_feat(partner)] + [to_feat(p) for p in chip_peers] + [to_grp(p) for p in grp_peers]
    for device in partners:
        pl.semaphore_signal(barrier, inc=1, device_id=device, device_id_type=MESH)
    pl.semaphore_wait(barrier, len(partners))

    near = 3 - 2 * core
    passed = 1 + 2 * core
    far = 4 - 4 * core
    other = 4 * core
    step = rows // CHUNKS
    chunks = [pl.ds(c * step, step) for c in range(CHUNKS)]
    if square:
        for c, at in enumerate(chunks):
            send(feat_hbm.at[at], pool.at[y_slot, at], halo_s.at[0, c], halo_r.at[y_slot, c], to_feat(x_peer))
    else:
        for c, at in enumerate(chunks):
            send(feat_hbm.at[at], pool.at[0, at], halo_s.at[0, c], halo_r.at[0, c], to_feat(ahead))
            send(feat_hbm.at[at], pool.at[4, at], halo_s.at[1, c], halo_r.at[4, c], to_feat(behind))
    send(feat_hbm, both.at[2], halo_s.at[2, 0], halo_r.at[SPAN, 0], to_feat(partner))

    dsum[...] = jnp.zeros_like(dsum)
    loads[0].wait()

    def build(piece, carry):
        owner = lax.rem(me + piece - SPAN + n_feat, n_feat)
        for b in range(num_blocks):
            dst_rows = slice(b * block_len, (b + 1) * block_len)
            for h in range(num_blocks):
                source = owner * num_blocks + h
                acc = jnp.zeros((block_len, block_len), jnp.float32)
                for k in range(num_slots):
                    hit = jnp.logical_and(src_ref[b, k] == source, cnt_ref[b] > k)
                    acc = acc + adj_ref[b, k].astype(jnp.float32) * jnp.where(hit, 1.0, 0.0)
                dsum[dst_rows, :] += acc
                dense[piece, dst_rows, h * block_len : (h + 1) * block_len] = acc.astype(jnp.bfloat16)
        return carry

    def relay():
        for c, at in enumerate(chunks):
            landed(pool.at[x_slot, at], halo_r.at[x_slot, c])
            if square:
                send(pool.at[x_slot, at], pool.at[y_slot, at], halo_s.at[1, c], halo_r.at[y_slot, c], to_feat(y_peer))

    lax.fori_loop(0, SPLIT, build, 0)
    relay()
    lax.fori_loop(SPLIT, WIN, build, 0)
    inv[...] = jnp.broadcast_to(lax.rsqrt(jnp.sum(dsum[...], axis=1, keepdims=True)), inv.shape)
    loads[1].wait()
    loads[2].wait()
    preact[...] = dot_nn(both[0], ws_ref[...])
    summed[...] = dot_nn(dense[SPAN], both[0])
    landed(both.at[2], halo_r.at[SPAN, 0])
    summed[...] += dot_nn(dense[near], both[2])
    summed[...] += dot_nn(dense[x_slot], pool[x_slot])
    for c, at in enumerate(chunks):
        landed(pool.at[y_slot, at], halo_r.at[y_slot, c])
        send(pool.at[far, at], pool.at[near, at], halo_s.at[3, c], halo_r.at[near, c], to_feat(partner))
    summed[...] += dot_nn(dense[y_slot], pool[y_slot])
    for load in loads[3:]:
        load.wait()
    for c, at in enumerate(chunks):
        landed(pool.at[passed, at], halo_r.at[passed, c])
    summed[...] += dot_nn(dense[passed], pool[passed])

    def aggregate(at):
        both[1, at, :] = (summed[at, :] * inv[at, :1]).astype(jnp.bfloat16)

    strips(rows, aggregate)
    send(both.at[1], both.at[3], pair_s.at[0], pair_r.at[0], to_feat(partner))
    preact[...] += dot_nn(both[1], wn_ref[...])
    mult_ref[...] = mult_ref[...] * jnp.exp2(-shift_ref[...].astype(jnp.float32))

    tstep = rows // 2
    halves = [pl.ds(c * tstep, tstep) for c in range(2)]

    def activate(at):
        scale = mult_ref[...]
        scaled = preact[at, :] * scale
        gate = 1.0 / (1.0 + jnp.exp(-scaled))
        out_ref[at, :] = (scaled * gate).astype(jnp.bfloat16)
        gpre[0, at, :] = (
            cot_ref[at, :].astype(jnp.float32) * gate * (1.0 + scaled * (1.0 - gate)) * scale
        ).astype(jnp.bfloat16)

    for c, at in enumerate(halves):
        strips(tstep, lambda part, c=c: activate(pl.ds(c * tstep + part.start, part.size)))
        send(gpre.at[0, at], gpre.at[1, at], pair_s.at[1 + c], pair_r.at[1 + c], to_feat(partner))
    stores = []

    def store(src, dst):
        copy = pltpu.make_async_copy(src, dst, store_s.at[len(stores)])
        copy.start()
        stores.append(copy)

    store(out_ref, out_hbm)

    pulled = dot_nt(gpre[0], wn_ref[...])
    back[...] = (pulled * inv[:, :1]).astype(jnp.bfloat16)
    term_out[passed] = dot_tn(dense[passed], back[...]).astype(jnp.bfloat16)
    send(term_out.at[passed], term_in.at[2], term_s.at[0, 0], term_r.at[2, 0], to_feat(partner))

    half = buf1.shape[0]
    c2 = buf2.shape[0]
    c3 = c2 // n_grp
    order = [lax.rem(chip + j, n_chip) for j in range(1, n_chip + 1)]
    if fine:
        owners = [lax.rem(grp + 1 + q, n_grp) for q in range(n_grp)]
        cuts = [(pl.multiple_of(o * c3, c3), c3) for o in owners]
    else:
        cuts = [(0, c2)]

    def share_out(j):
        for q, (first, size) in enumerate(cuts):
            src = buf1.at[pl.ds(pl.multiple_of(order[j] * c2 + first, 16), size)]
            send(src, in2.at[j, pl.ds(first, size)], rs2_s.at[j, q], rs2_r.at[j, q], to_feat(chip_peers[j]))

    landed(both.at[3], pair_r.at[0])
    for c, at in enumerate(halves):
        landed(gpre.at[1, at], pair_r.at[1 + c])
    if lanes == gpre.shape[2]:
        for j in range(n_chip):
            at = pl.ds(pl.multiple_of(order[j] * c2, c2), c2)
            part = dot_tn(both[core, :, at], gpre[0]) + dot_tn(both[2 + core, :, at], gpre[1])
            buf1[at, :] = part.astype(jnp.bfloat16)
            if j < n_chip - 1:
                share_out(j)
    else:
        part = dot_tn(both[core], gpre[0]) + dot_tn(both[2 + core], gpre[1])
        for j in range(gpre.shape[2] // lanes):
            buf1[j * width : (j + 1) * width, :] = part[:, j * lanes : (j + 1) * lanes].astype(jnp.bfloat16)
        for j in range(n_chip - 1):
            share_out(j)

    term_sum[0] = dot_tn(dense[x_slot], back[...])
    term_sum[1] = dot_tn(dense[y_slot], back[...])
    landed(term_in.at[2], term_r.at[2, 0])
    through = lax.rem(core + chip, 2)
    term_sum[through] += term_in[2].astype(jnp.float32)
    for c, at in enumerate(halves):
        term_out[y_slot, at, :] = term_sum[1, at, :].astype(jnp.bfloat16)
        if square:
            send(term_out.at[y_slot, at], term_in.at[1, at], term_s.at[1, c], term_r.at[1, c], to_feat(y_peer))
        else:
            target = lax.rem(me + y_slot - 2 + n_feat, n_feat)
            send(term_out.at[y_slot, at], term_in.at[odd, at], term_s.at[1, c], term_r.at[odd, c], to_feat(target))
    term_out[near] = dot_tn(dense[near], back[...]).astype(jnp.bfloat16)
    send(term_out.at[near], term_in.at[3], term_s.at[3, 0], term_r.at[3, 0], to_feat(partner))
    own_grad[...] = dot_nt(gpre[0], ws_ref[...])
    own_grad[...] += dot_tn(dense[SPAN], back[...])

    def send_terms():
        for c, at in enumerate(halves):
            value = term_sum[0, at, :]
            if square:
                landed(term_in.at[1, at], term_r.at[1, c])
                value = value + term_in[1, at, :].astype(jnp.float32)
            term_out[x_slot, at, :] = value.astype(jnp.bfloat16)
            if square:
                send(term_out.at[x_slot, at], term_in.at[0, at], term_s.at[2, c], term_r.at[0, c], to_feat(x_peer))
            else:
                target = lax.rem(me + x_slot - 2 + n_feat, n_feat)
                place = 1 - odd
                send(term_out.at[x_slot, at], term_in.at[place, at], term_s.at[2, c], term_r.at[place, c], to_feat(target))

    if not fine:
        send_terms()

    for q, (first, size) in enumerate(cuts):
        at = pl.ds(first, size)
        total = buf1[pl.ds(pl.multiple_of(chip * c2 + first, 16), size), :].astype(jnp.float32)
        for j in range(n_chip - 1):
            landed(in2.at[j, at], rs2_r.at[j, q])
            total = total + in2[j, at, :].astype(jnp.float32)
        buf2[at, :] = total.astype(jnp.bfloat16)
        if fine and q < n_grp - 1:
            send(buf2.at[at], in3.at[q], rs3_s.at[q], rs3_r.at[q], to_grp(grp_peers[q]))
    if fine:
        send_terms()
    else:
        for j, peer in enumerate(grp_peers):
            at = pl.ds(pl.multiple_of(peer * c3, c3), c3)
            send(buf2.at[at], in3.at[j], rs3_s.at[j], rs3_r.at[j], to_grp(peer))
    total = buf2[pl.ds(pl.multiple_of(grp * c3, c3), c3), :].astype(jnp.float32)
    for j in range(n_grp - 1):
        landed(in3.at[j], rs3_r.at[j])
        total = total + in3[j].astype(jnp.float32)

    def piece3(owner):
        return full.at[pl.ds(pl.multiple_of(core * half + chip * c2 + owner * c3, c3), c3)]

    def piece2(side, owner):
        return full.at[pl.ds(pl.multiple_of(side * half + owner * c2, c2), c2)]

    def spread_piece(owner, q):
        for j, peer in enumerate((x_peer, y_peer) if square else chip_peers):
            send(piece3(owner), piece3(owner), ag2_s.at[j, q], ag2_r.at[j, q], to_feat(peer))

    piece3(grp)[...] = total.astype(jnp.bfloat16)
    for j, peer in enumerate(grp_peers):
        send(piece3(grp), piece3(grp), ag3_s.at[j], ag3_r.at[j], to_grp(peer))
    if fine:
        spread_piece(grp, 0)
    for j in range(n_grp - 1):
        owner = lax.rem(grp + n_grp - 1 - j, n_grp)
        landed(piece3(owner), ag3_r.at[j])
        if fine:
            spread_piece(owner, j + 1)
    if not fine:
        for j, peer in enumerate(chip_peers):
            send(piece2(core, chip), piece2(core, chip), ag2_s.at[j, 0], ag2_r.at[j, 0], to_feat(peer))
    send(piece2(core, chip), piece2(core, chip), ag1_s.at[0], ag1_r.at[0], to_feat(partner))

    def piece_of(owner, q):
        if not fine:
            return piece2(core, owner)
        first = core * half + owner * c2 + lax.rem(grp + n_grp - q, n_grp) * c3
        return full.at[pl.ds(pl.multiple_of(first, c3), c3)]

    if square:
        sources = [x_peer // 2, y_peer // 2, lax.rem(x_peer // 2 + 2, n_chip)]
        for q in range(len(cuts)):
            for j in range(2):
                landed(piece_of(sources[j], q), ag2_r.at[j, q])
                if j == q % 2:
                    piece = piece_of(sources[j], q)
                    send(piece, piece, ag2_s.at[2, q], ag2_r.at[2, q], to_feat((y_peer, x_peer)[j]))
        for j in range(2):
            place = piece2(core, sources[j])
            send(place, place, ag1_s.at[j + 1], ag1_r.at[j + 1], to_feat(partner))
    else:
        sources = [lax.rem(chip + n_chip - 1 - j, n_chip) for j in range(n_chip - 1)]

    arrivals = (0, 3) if square else (0, 1, 3)
    for slot in arrivals:
        if slot == 3:
            landed(term_in.at[3], term_r.at[3, 0])
        else:
            for c, at in enumerate(halves):
                landed(term_in.at[slot, at], term_r.at[slot, c])

    def finish(at):
        grad = own_grad[at, :]
        for slot in arrivals:
            grad = grad + term_in[slot, at, :].astype(jnp.float32)
        gfeat_ref[at, :] = grad.astype(jnp.bfloat16)

    strips(rows, finish)
    store(gfeat_ref, gfeat_hbm)

    for j in range(2 if square else 0, n_chip - 1):
        for q in range(len(cuts)):
            landed(piece_of(sources[j], q), ag2_r.at[j, q])
        place = piece2(core, sources[j])
        send(place, place, ag1_s.at[j + 1], ag1_r.at[j + 1], to_feat(partner))
    own_half = pl.ds(pl.multiple_of(core * half, half), half)
    store(full.at[own_half], grads_hbm.at[own_half])
    for j, owner in enumerate([chip] + sources):
        landed(piece2(1 - core, owner), ag1_r.at[j])
    its_half = pl.ds(pl.multiple_of((1 - core) * half, half), half)
    store(full.at[its_half], grads_hbm.at[its_half])
    for copy in sent:
        copy.wait_send()
    for copy in stores:
        copy.wait()


def place_outputs(
    grad_scale, out_in, gfeat_in, grads_in, out_hbm, gfeat_hbm, self_hbm, neigh_hbm, held, scaled, load_s, store_s
):
    part = held.shape[1]
    loads = [
        pltpu.make_async_copy(grads_in.at[pl.ds(i * part, part)], held.at[i], load_s.at[i]) for i in range(4)
    ]
    moves = [
        pltpu.make_async_copy(out_in, out_hbm, store_s.at[4]),
        pltpu.make_async_copy(gfeat_in, gfeat_hbm, store_s.at[5]),
    ]
    for copy in loads + moves:
        copy.start()
    for i in range(4):
        loads[i].wait()

        def widen(at, i=i):
            scaled[i, at, :] = held[i, at, :].astype(jnp.float32) * grad_scale

        strips(part, widen, 64)
        dst = (self_hbm, neigh_hbm)[i // 2].at[pl.ds((i % 2) * part, part)]
        store = pltpu.make_async_copy(scaled.at[i], dst, store_s.at[i])
        store.start()
        moves.append(store)
    for copy in moves:
        copy.wait()


def local(
    n_feat, n_grp, features, adj_tiles, src_block, counts, w_self, w_neigh, multiplier, bit_shift, cotangent
):
    rows, width = features.shape
    hidden = w_self.shape[1]
    n_chip = n_feat // 2
    lanes = hidden if width % (16 * n_chip * n_grp) == 0 else 128
    fine = n_chip * n_grp <= 16
    half = width * hidden // lanes
    c2 = half // n_chip
    c3 = c2 // n_grp
    bf, f32 = jnp.bfloat16, jnp.float32
    smem = pl.BlockSpec(memory_space=pltpu.SMEM)
    hbm = pl.BlockSpec(memory_space=pltpu.HBM)
    dma = pltpu.SemaphoreType.DMA
    cuts = n_grp if fine else 1
    output, grad_features, grads = pl.pallas_call(
        functools.partial(kernel, n_feat, n_grp, fine),
        out_shape=(
            jax.ShapeDtypeStruct((rows, hidden), bf),
            jax.ShapeDtypeStruct((rows, width), bf),
            jax.ShapeDtypeStruct((2 * half, lanes), bf),
        ),
        in_specs=[smem, smem] + [hbm] * 7,
        out_specs=(hbm, hbm, hbm),
        scratch_shapes=[
            pltpu.VMEM((rows, hidden), bf),
            pltpu.VMEM((rows, width), bf),
            pltpu.VMEM(adj_tiles.shape, bf),
            pltpu.VMEM(w_self.shape, bf),
            pltpu.VMEM(w_neigh.shape, bf),
            pltpu.VMEM((1, hidden), f32),
            pltpu.VMEM((1, hidden), jnp.int32),
            pltpu.VMEM((rows, hidden), bf),
            pltpu.VMEM((WIN, rows, width), bf),
            pltpu.VMEM((WIN, rows, rows), bf),
            pltpu.VMEM((rows, adj_tiles.shape[3]), f32),
            pltpu.VMEM((rows, 128), f32),
            pltpu.VMEM((rows, width), f32),
            pltpu.VMEM((rows, hidden), f32),
            pltpu.VMEM((4, rows, width), bf),
            pltpu.VMEM((2, rows, hidden), bf),
            pltpu.VMEM((half, lanes), bf),
            pltpu.VMEM((n_chip - 1, c2, lanes), bf),
            pltpu.VMEM((c2, lanes), bf),
            pltpu.VMEM((n_grp - 1, c3, lanes), bf),
            pltpu.VMEM((2 * half, lanes), bf),
            pltpu.VMEM((rows, width), bf),
            pltpu.VMEM((WIN, rows, width), bf),
            pltpu.VMEM((2, rows, width), f32),
            pltpu.VMEM((rows, width), f32),
            pltpu.VMEM((4, rows, width), bf),
            dma((7,)), dma((4,)), dma((4, CHUNKS)), dma((WIN, CHUNKS)), dma((4, 2)), dma((4, 2)),
            dma((3,)), dma((3,)), dma((n_chip - 1, cuts)), dma((n_chip - 1, cuts)),
            dma((n_grp - 1,)), dma((n_grp - 1,)),
            dma((n_chip,)), dma((n_chip,)), dma((n_chip - 1, cuts)), dma((n_chip - 1, cuts)),
            dma((n_grp - 1,)), dma((n_grp - 1,)),
        ],
        compiler_params=pltpu.CompilerParams(
            collective_id=0, has_side_effects=True, vmem_limit_bytes=62 * 1024 * 1024
        ),
    )(
        src_block, counts, features, adj_tiles, w_self, w_neigh,
        multiplier.reshape(1, hidden), bit_shift.reshape(1, hidden), cotangent,
    )
    grad_scale = 1.0 / math.sqrt(rows * n_grp * n_feat)
    if lanes != hidden:
        grads = grads.reshape(2, hidden // lanes, width, lanes).transpose(0, 2, 1, 3).reshape(2 * width, hidden)
    return pl.pallas_call(
        functools.partial(place_outputs, grad_scale),
        out_shape=(
            jax.ShapeDtypeStruct(output.shape, bf),
            jax.ShapeDtypeStruct(grad_features.shape, bf),
            jax.ShapeDtypeStruct((width, hidden), f32),
            jax.ShapeDtypeStruct((width, hidden), f32),
        ),
        in_specs=[hbm] * 3,
        out_specs=(hbm,) * 4,
        scratch_shapes=[
            pltpu.VMEM((4, width // 2, hidden), bf),
            pltpu.VMEM((4, width // 2, hidden), f32),
            dma((4,)),
            dma((6,)),
        ],
        compiler_params=pltpu.CompilerParams(vmem_limit_bytes=62 * 1024 * 1024),
    )(output, grad_features, grads)


def solution(mesh):
    return jax.shard_map(
        functools.partial(local, mesh.shape["feat"], mesh.shape["grp"]),
        mesh=mesh,
        in_specs=(
            P(("grp", "feat"), None),
            P(("grp", "feat"), None, None, None),
            P(("grp", "feat"), None),
            P(("grp", "feat")),
            P(),
            P(),
            P(),
            P(),
            P(("grp", "feat"), None),
        ),
        out_specs=(P(("grp", "feat"), None), P(("grp", "feat"), None), P(), P()),
        check_vma=False,
    )
```

```python
import functools
import math

import jax
import jax.numpy as jnp
from jax import lax
from jax.experimental import pallas as pl
from jax.experimental.pallas import tpu as pltpu
from jax.sharding import PartitionSpec as P

SPAN = 2
WIN = 2 * SPAN + 1
MESH = pl.DeviceIdType.MESH
STRIP = 32
CHUNKS = 8
SPLIT = 3


def dot_nn(a, b):
    return jnp.dot(a, b, preferred_element_type=jnp.float32)


def dot_tn(a, b):
    return lax.dot_general(a, b, (((0,), (0,)), ((), ())), preferred_element_type=jnp.float32)


def dot_nt(a, b):
    return lax.dot_general(a, b, (((1,), (1,)), ((), ())), preferred_element_type=jnp.float32)


def strips(rows, body, step=STRIP):
    def run(i, carry):
        body(pl.ds(pl.multiple_of(i * step, step), step))
        return carry

    lax.fori_loop(0, rows // step, run, 0)


def kernel(
    n_feat, n_grp, fine,
    src_ref, cnt_ref, feat_hbm, adj_hbm, ws_hbm, wn_hbm, mult_hbm, shift_hbm, cot_hbm,
    out_hbm, gfeat_hbm, grads_hbm,
    out_ref, gfeat_ref,
    adj_ref, ws_ref, wn_ref, mult_ref, shift_ref, cot_ref,
    pool, dense, dsum, inv, summed, preact, both, gpre,
    buf1, in2, buf2, in3, full,
    back, term_out, term_sum, own_grad, term_in,
    load_s, store_s, halo_s, halo_r, term_s, term_r,
    pair_s, pair_r, rs2_s, rs2_r, rs3_s, rs3_r,
    ag1_s, ag1_r, ag2_s, ag2_r, ag3_s, ag3_r,
):
    n_chip = n_feat // 2
    square = n_chip == 4
    me = lax.axis_index("feat")
    grp = lax.axis_index("grp")
    core = lax.rem(me, 2)
    chip = me // 2
    odd = lax.rem(chip, 2)
    partner = me + 1 - 2 * core
    num_blocks, num_slots, block_len, _ = adj_ref.shape
    rows, width = feat_hbm.shape
    lanes = buf1.shape[1]
    ahead = lax.rem(me + 2, n_feat)
    behind = lax.rem(me + n_feat - 2, n_feat)
    chip_peers = [2 * lax.rem(chip + j, n_chip) + core for j in range(1, n_chip)]
    grp_peers = [lax.rem(grp + j, n_grp) for j in range(1, n_grp)]
    x_slot = 4 - 4 * odd
    y_slot = 4 * odd
    x_peer = 2 * (chip + 1 - 2 * odd) + core
    y_peer = 2 * lax.rem(chip + 2, n_chip) + core

    def to_feat(peer):
        return (grp, peer)

    def to_grp(peer):
        return (peer, me)

    sent = []

    def send(src, dst, ssem, rsem, device):
        copy = pltpu.make_async_remote_copy(
            src_ref=src, dst_ref=dst, send_sem=ssem, recv_sem=rsem, device_id=device, device_id_type=MESH
        )
        copy.start()
        sent.append(copy)

    def landed(dst, rsem):
        pltpu.make_async_remote_copy(
            src_ref=dst, dst_ref=dst, send_sem=rsem, recv_sem=rsem, device_id=to_feat(partner), device_id_type=MESH
        ).wait_recv()

    loads = [
        pltpu.make_async_copy(src, dst, load_s.at[i])
        for i, (src, dst) in enumerate(
            (
                (feat_hbm, both.at[0]), (adj_hbm, adj_ref), (ws_hbm, ws_ref), (wn_hbm, wn_ref),
                (mult_hbm, mult_ref), (shift_hbm, shift_ref), (cot_hbm, cot_ref),
            )
        )
    ]
    barrier = pltpu.get_barrier_semaphore()
    partners = [to_feat(partner)] + [to_feat(p) for p in chip_peers] + [to_grp(p) for p in grp_peers]
    for device in partners:
        pl.semaphore_signal(barrier, inc=1, device_id=device, device_id_type=MESH)
    for load in loads:
        load.start()
    loads[0].wait()
    pl.semaphore_wait(barrier, len(partners))

    near = 3 - 2 * core
    passed = 1 + 2 * core
    far = 4 - 4 * core
    other = 4 * core
    step = rows // CHUNKS
    chunks = [pl.ds(c * step, step) for c in range(CHUNKS)]
    if square:
        for c, at in enumerate(chunks):
            send(both.at[0, at], pool.at[y_slot, at], halo_s.at[0, c], halo_r.at[y_slot, c], to_feat(x_peer))
    else:
        for c, at in enumerate(chunks):
            send(both.at[0, at], pool.at[0, at], halo_s.at[0, c], halo_r.at[0, c], to_feat(ahead))
            send(both.at[0, at], pool.at[4, at], halo_s.at[1, c], halo_r.at[4, c], to_feat(behind))
    send(both.at[0], both.at[2], halo_s.at[2, 0], halo_r.at[SPAN, 0], to_feat(partner))

    dsum[...] = jnp.zeros_like(dsum)
    loads[1].wait()

    def build(piece, carry):
        owner = lax.rem(me + piece - SPAN + n_feat, n_feat)
        for b in range(num_blocks):
            dst_rows = slice(b * block_len, (b + 1) * block_len)
            for h in range(num_blocks):
                source = owner * num_blocks + h
                acc = jnp.zeros((block_len, block_len), jnp.float32)
                for k in range(num_slots):
                    hit = jnp.logical_and(src_ref[b, k] == source, cnt_ref[b] > k)
                    acc = acc + adj_ref[b, k].astype(jnp.float32) * jnp.where(hit, 1.0, 0.0)
                dsum[dst_rows, :] += acc
                dense[piece, dst_rows, h * block_len : (h + 1) * block_len] = acc.astype(jnp.bfloat16)
        return carry

    def relay():
        for c, at in enumerate(chunks):
            landed(pool.at[x_slot, at], halo_r.at[x_slot, c])
            if square:
                send(pool.at[x_slot, at], pool.at[y_slot, at], halo_s.at[1, c], halo_r.at[y_slot, c], to_feat(y_peer))

    lax.fori_loop(0, SPLIT, build, 0)
    relay()
    lax.fori_loop(SPLIT, WIN, build, 0)
    inv[...] = jnp.broadcast_to(lax.rsqrt(jnp.sum(dsum[...], axis=1, keepdims=True)), inv.shape)
    loads[2].wait()
    preact[...] = dot_nn(both[0], ws_ref[...])
    summed[...] = dot_nn(dense[SPAN], both[0])
    landed(both.at[2], halo_r.at[SPAN, 0])
    summed[...] += dot_nn(dense[near], both[2])
    summed[...] += dot_nn(dense[x_slot], pool[x_slot])
    for c, at in enumerate(chunks):
        landed(pool.at[y_slot, at], halo_r.at[y_slot, c])
        send(pool.at[far, at], pool.at[near, at], halo_s.at[3, c], halo_r.at[near, c], to_feat(partner))
    summed[...] += dot_nn(dense[y_slot], pool[y_slot])
    for load in loads[3:]:
        load.wait()
    for c, at in enumerate(chunks):
        landed(pool.at[passed, at], halo_r.at[passed, c])
    summed[...] += dot_nn(dense[passed], pool[passed])

    def aggregate(at):
        both[1, at, :] = (summed[at, :] * inv[at, :1]).astype(jnp.bfloat16)

    strips(rows, aggregate)
    send(both.at[1], both.at[3], pair_s.at[0], pair_r.at[0], to_feat(partner))
    preact[...] += dot_nn(both[1], wn_ref[...])
    mult_ref[...] = mult_ref[...] * jnp.exp2(-shift_ref[...].astype(jnp.float32))

    tstep = rows // 2
    halves = [pl.ds(c * tstep, tstep) for c in range(2)]

    def activate(at):
        scale = mult_ref[...]
        scaled = preact[at, :] * scale
        gate = 1.0 / (1.0 + jnp.exp(-scaled))
        out_ref[at, :] = (scaled * gate).astype(jnp.bfloat16)
        gpre[0, at, :] = (
            cot_ref[at, :].astype(jnp.float32) * gate * (1.0 + scaled * (1.0 - gate)) * scale
        ).astype(jnp.bfloat16)

    for c, at in enumerate(halves):
        strips(tstep, lambda part, c=c: activate(pl.ds(c * tstep + part.start, part.size)))
        send(gpre.at[0, at], gpre.at[1, at], pair_s.at[1 + c], pair_r.at[1 + c], to_feat(partner))
    stores = []

    def store(src, dst):
        copy = pltpu.make_async_copy(src, dst, store_s.at[len(stores)])
        copy.start()
        stores.append(copy)

    store(out_ref, out_hbm)

    pulled = dot_nt(gpre[0], wn_ref[...])
    back[...] = (pulled * inv[:, :1]).astype(jnp.bfloat16)
    term_out[passed] = dot_tn(dense[passed], back[...]).astype(jnp.bfloat16)
    send(term_out.at[passed], term_in.at[2], term_s.at[0, 0], term_r.at[2, 0], to_feat(partner))

    half = buf1.shape[0]
    c2 = buf2.shape[0]
    c3 = c2 // n_grp
    order = [lax.rem(chip + j, n_chip) for j in range(1, n_chip + 1)]
    if fine:
        owners = [lax.rem(grp + 1 + q, n_grp) for q in range(n_grp)]
        cuts = [(pl.multiple_of(o * c3, c3), c3) for o in owners]
    else:
        cuts = [(0, c2)]

    def share_out(j):
        for q, (first, size) in enumerate(cuts):
            src = buf1.at[pl.ds(pl.multiple_of(order[j] * c2 + first, 16), size)]
            send(src, in2.at[j, pl.ds(first, size)], rs2_s.at[j, q], rs2_r.at[j, q], to_feat(chip_peers[j]))

    landed(both.at[3], pair_r.at[0])
    for c, at in enumerate(halves):
        landed(gpre.at[1, at], pair_r.at[1 + c])
    if lanes == gpre.shape[2]:
        for j in range(n_chip):
            at = pl.ds(pl.multiple_of(order[j] * c2, c2), c2)
            part = dot_tn(both[core, :, at], gpre[0]) + dot_tn(both[2 + core, :, at], gpre[1])
            buf1[at, :] = part.astype(jnp.bfloat16)
            if j < n_chip - 1:
                share_out(j)
    else:
        part = dot_tn(both[core], gpre[0]) + dot_tn(both[2 + core], gpre[1])
        for j in range(gpre.shape[2] // lanes):
            buf1[j * width : (j + 1) * width, :] = part[:, j * lanes : (j + 1) * lanes].astype(jnp.bfloat16)
        for j in range(n_chip - 1):
            share_out(j)

    term_sum[0] = dot_tn(dense[x_slot], back[...])
    term_sum[1] = dot_tn(dense[y_slot], back[...])
    landed(term_in.at[2], term_r.at[2, 0])
    through = lax.rem(core + chip, 2)
    term_sum[through] += term_in[2].astype(jnp.float32)
    for c, at in enumerate(halves):
        term_out[y_slot, at, :] = term_sum[1, at, :].astype(jnp.bfloat16)
        if square:
            send(term_out.at[y_slot, at], term_in.at[1, at], term_s.at[1, c], term_r.at[1, c], to_feat(y_peer))
        else:
            target = lax.rem(me + y_slot - 2 + n_feat, n_feat)
            send(term_out.at[y_slot, at], term_in.at[odd, at], term_s.at[1, c], term_r.at[odd, c], to_feat(target))
    term_out[near] = dot_tn(dense[near], back[...]).astype(jnp.bfloat16)
    send(term_out.at[near], term_in.at[3], term_s.at[3, 0], term_r.at[3, 0], to_feat(partner))
    own_grad[...] = dot_nt(gpre[0], ws_ref[...])
    own_grad[...] += dot_tn(dense[SPAN], back[...])

    def send_terms():
        for c, at in enumerate(halves):
            value = term_sum[0, at, :]
            if square:
                landed(term_in.at[1, at], term_r.at[1, c])
                value = value + term_in[1, at, :].astype(jnp.float32)
            term_out[x_slot, at, :] = value.astype(jnp.bfloat16)
            if square:
                send(term_out.at[x_slot, at], term_in.at[0, at], term_s.at[2, c], term_r.at[0, c], to_feat(x_peer))
            else:
                target = lax.rem(me + x_slot - 2 + n_feat, n_feat)
                place = 1 - odd
                send(term_out.at[x_slot, at], term_in.at[place, at], term_s.at[2, c], term_r.at[place, c], to_feat(target))

    if not fine:
        send_terms()

    for q, (first, size) in enumerate(cuts):
        at = pl.ds(first, size)
        total = buf1[pl.ds(pl.multiple_of(chip * c2 + first, 16), size), :].astype(jnp.float32)
        for j in range(n_chip - 1):
            landed(in2.at[j, at], rs2_r.at[j, q])
            total = total + in2[j, at, :].astype(jnp.float32)
        buf2[at, :] = total.astype(jnp.bfloat16)
        if fine and q < n_grp - 1:
            send(buf2.at[at], in3.at[q], rs3_s.at[q], rs3_r.at[q], to_grp(grp_peers[q]))
    if fine:
        send_terms()
    else:
        for j, peer in enumerate(grp_peers):
            at = pl.ds(pl.multiple_of(peer * c3, c3), c3)
            send(buf2.at[at], in3.at[j], rs3_s.at[j], rs3_r.at[j], to_grp(peer))
    total = buf2[pl.ds(pl.multiple_of(grp * c3, c3), c3), :].astype(jnp.float32)
    for j in range(n_grp - 1):
        landed(in3.at[j], rs3_r.at[j])
        total = total + in3[j].astype(jnp.float32)

    def piece3(owner):
        return full.at[pl.ds(pl.multiple_of(core * half + chip * c2 + owner * c3, c3), c3)]

    def piece2(side, owner):
        return full.at[pl.ds(pl.multiple_of(side * half + owner * c2, c2), c2)]

    def spread_piece(owner, q):
        for j, peer in enumerate((x_peer, y_peer) if square else chip_peers):
            send(piece3(owner), piece3(owner), ag2_s.at[j, q], ag2_r.at[j, q], to_feat(peer))

    piece3(grp)[...] = total.astype(jnp.bfloat16)
    for j, peer in enumerate(grp_peers):
        send(piece3(grp), piece3(grp), ag3_s.at[j], ag3_r.at[j], to_grp(peer))
    if fine:
        spread_piece(grp, 0)
    for j in range(n_grp - 1):
        owner = lax.rem(grp + n_grp - 1 - j, n_grp)
        landed(piece3(owner), ag3_r.at[j])
        if fine:
            spread_piece(owner, j + 1)
    if not fine:
        for j, peer in enumerate(chip_peers):
            send(piece2(core, chip), piece2(core, chip), ag2_s.at[j, 0], ag2_r.at[j, 0], to_feat(peer))
    send(piece2(core, chip), piece2(core, chip), ag1_s.at[0], ag1_r.at[0], to_feat(partner))

    def piece_of(owner, q):
        if not fine:
            return piece2(core, owner)
        first = core * half + owner * c2 + lax.rem(grp + n_grp - q, n_grp) * c3
        return full.at[pl.ds(pl.multiple_of(first, c3), c3)]

    if square:
        sources = [x_peer // 2, y_peer // 2, lax.rem(x_peer // 2 + 2, n_chip)]
        for q in range(len(cuts)):
            for j in range(2):
                landed(piece_of(sources[j], q), ag2_r.at[j, q])
                if j == q % 2:
                    piece = piece_of(sources[j], q)
                    send(piece, piece, ag2_s.at[2, q], ag2_r.at[2, q], to_feat((y_peer, x_peer)[j]))
        for j in range(2):
            place = piece2(core, sources[j])
            send(place, place, ag1_s.at[j + 1], ag1_r.at[j + 1], to_feat(partner))
    else:
        sources = [lax.rem(chip + n_chip - 1 - j, n_chip) for j in range(n_chip - 1)]

    arrivals = (0, 3) if square else (0, 1, 3)
    for slot in arrivals:
        if slot == 3:
            landed(term_in.at[3], term_r.at[3, 0])
        else:
            for c, at in enumerate(halves):
                landed(term_in.at[slot, at], term_r.at[slot, c])

    def finish(at):
        grad = own_grad[at, :]
        for slot in arrivals:
            grad = grad + term_in[slot, at, :].astype(jnp.float32)
        gfeat_ref[at, :] = grad.astype(jnp.bfloat16)

    strips(rows, finish)
    store(gfeat_ref, gfeat_hbm)

    for j in range(2 if square else 0, n_chip - 1):
        for q in range(len(cuts)):
            landed(piece_of(sources[j], q), ag2_r.at[j, q])
        place = piece2(core, sources[j])
        send(place, place, ag1_s.at[j + 1], ag1_r.at[j + 1], to_feat(partner))
    own_half = pl.ds(pl.multiple_of(core * half, half), half)
    store(full.at[own_half], grads_hbm.at[own_half])
    for j, owner in enumerate([chip] + sources):
        landed(piece2(1 - core, owner), ag1_r.at[j])
    its_half = pl.ds(pl.multiple_of((1 - core) * half, half), half)
    store(full.at[its_half], grads_hbm.at[its_half])
    for copy in sent:
        copy.wait_send()
    for copy in stores:
        copy.wait()


def place_outputs(
    grad_scale, out_in, gfeat_in, grads_in, out_hbm, gfeat_hbm, self_hbm, neigh_hbm,
    held, scaled, out_held, gfeat_held, load_s, store_s
):
    part = held.shape[1]
    loads = [
        pltpu.make_async_copy(grads_in.at[pl.ds(i * part, part)], held.at[i], load_s.at[i]) for i in range(4)
    ]
    fetches = [
        pltpu.make_async_copy(out_in, out_held, load_s.at[4]),
        pltpu.make_async_copy(gfeat_in, gfeat_held, load_s.at[5]),
    ]
    for copy in loads + fetches:
        copy.start()
    moves = []
    for i in range(4):
        loads[i].wait()

        def widen(at, i=i):
            scaled[i, at, :] = held[i, at, :].astype(jnp.float32) * grad_scale

        strips(part, widen, 64)
        dst = (self_hbm, neigh_hbm)[i // 2].at[pl.ds((i % 2) * part, part)]
        store = pltpu.make_async_copy(scaled.at[i], dst, store_s.at[i])
        store.start()
        moves.append(store)
    for i, (src, dst) in enumerate(((out_held, out_hbm), (gfeat_held, gfeat_hbm))):
        fetches[i].wait()
        move = pltpu.make_async_copy(src, dst, store_s.at[4 + i])
        move.start()
        moves.append(move)
    for copy in moves:
        copy.wait()


def local(
    n_feat, n_grp, features, adj_tiles, src_block, counts, w_self, w_neigh, multiplier, bit_shift, cotangent
):
    rows, width = features.shape
    hidden = w_self.shape[1]
    n_chip = n_feat // 2
    lanes = hidden if width % (16 * n_chip * n_grp) == 0 else 128
    fine = n_chip * n_grp <= 16
    half = width * hidden // lanes
    c2 = half // n_chip
    c3 = c2 // n_grp
    bf, f32 = jnp.bfloat16, jnp.float32
    smem = pl.BlockSpec(memory_space=pltpu.SMEM)
    hbm = pl.BlockSpec(memory_space=pltpu.HBM)
    dma = pltpu.SemaphoreType.DMA
    cuts = n_grp if fine else 1
    output, grad_features, grads = pl.pallas_call(
        functools.partial(kernel, n_feat, n_grp, fine),
        out_shape=(
            jax.ShapeDtypeStruct((rows, hidden), bf),
            jax.ShapeDtypeStruct((rows, width), bf),
            jax.ShapeDtypeStruct((2 * half, lanes), bf),
        ),
        in_specs=[smem, smem] + [hbm] * 7,
        out_specs=(hbm, hbm, hbm),
        scratch_shapes=[
            pltpu.VMEM((rows, hidden), bf),
            pltpu.VMEM((rows, width), bf),
            pltpu.VMEM(adj_tiles.shape, bf),
            pltpu.VMEM(w_self.shape, bf),
            pltpu.VMEM(w_neigh.shape, bf),
            pltpu.VMEM((1, hidden), f32),
            pltpu.VMEM((1, hidden), jnp.int32),
            pltpu.VMEM((rows, hidden), bf),
            pltpu.VMEM((WIN, rows, width), bf),
            pltpu.VMEM((WIN, rows, rows), bf),
            pltpu.VMEM((rows, adj_tiles.shape[3]), f32),
            pltpu.VMEM((rows, 128), f32),
            pltpu.VMEM((rows, width), f32),
            pltpu.VMEM((rows, hidden), f32),
            pltpu.VMEM((4, rows, width), bf),
            pltpu.VMEM((2, rows, hidden), bf),
            pltpu.VMEM((half, lanes), bf),
            pltpu.VMEM((n_chip - 1, c2, lanes), bf),
            pltpu.VMEM((c2, lanes), bf),
            pltpu.VMEM((n_grp - 1, c3, lanes), bf),
            pltpu.VMEM((2 * half, lanes), bf),
            pltpu.VMEM((rows, width), bf),
            pltpu.VMEM((WIN, rows, width), bf),
            pltpu.VMEM((2, rows, width), f32),
            pltpu.VMEM((rows, width), f32),
            pltpu.VMEM((4, rows, width), bf),
            dma((7,)), dma((4,)), dma((4, CHUNKS)), dma((WIN, CHUNKS)), dma((4, 2)), dma((4, 2)),
            dma((3,)), dma((3,)), dma((n_chip - 1, cuts)), dma((n_chip - 1, cuts)),
            dma((n_grp - 1,)), dma((n_grp - 1,)),
            dma((n_chip,)), dma((n_chip,)), dma((n_chip - 1, cuts)), dma((n_chip - 1, cuts)),
            dma((n_grp - 1,)), dma((n_grp - 1,)),
        ],
        compiler_params=pltpu.CompilerParams(
            collective_id=0, has_side_effects=True, vmem_limit_bytes=62 * 1024 * 1024
        ),
    )(
        src_block, counts, features, adj_tiles, w_self, w_neigh,
        multiplier.reshape(1, hidden), bit_shift.reshape(1, hidden), cotangent,
    )
    grad_scale = 1.0 / math.sqrt(rows * n_grp * n_feat)
    if lanes != hidden:
        grads = grads.reshape(2, hidden // lanes, width, lanes).transpose(0, 2, 1, 3).reshape(2 * width, hidden)
    return pl.pallas_call(
        functools.partial(place_outputs, grad_scale),
        out_shape=(
            jax.ShapeDtypeStruct(output.shape, bf),
            jax.ShapeDtypeStruct(grad_features.shape, bf),
            jax.ShapeDtypeStruct((width, hidden), f32),
            jax.ShapeDtypeStruct((width, hidden), f32),
        ),
        in_specs=[hbm] * 3,
        out_specs=(hbm,) * 4,
        scratch_shapes=[
            pltpu.VMEM((4, width // 2, hidden), bf),
            pltpu.VMEM((4, width // 2, hidden), f32),
            pltpu.VMEM(output.shape, bf),
            pltpu.VMEM(grad_features.shape, bf),
            dma((6,)),
            dma((6,)),
        ],
        compiler_params=pltpu.CompilerParams(vmem_limit_bytes=62 * 1024 * 1024),
    )(output, grad_features, grads)


def solution(mesh):
    return jax.shard_map(
        functools.partial(local, mesh.shape["feat"], mesh.shape["grp"]),
        mesh=mesh,
        in_specs=(
            P(("grp", "feat"), None),
            P(("grp", "feat"), None, None, None),
            P(("grp", "feat"), None),
            P(("grp", "feat")),
            P(),
            P(),
            P(),
            P(),
            P(("grp", "feat"), None),
        ),
        out_specs=(P(("grp", "feat"), None), P(("grp", "feat"), None), P(), P()),
        check_vma=False,
    )
```

```python
import functools
import math

import jax
import jax.numpy as jnp
from jax import lax
from jax.experimental import pallas as pl
from jax.experimental.pallas import tpu as pltpu
from jax.sharding import PartitionSpec as P

SPAN = 2
WIN = 2 * SPAN + 1
MESH = pl.DeviceIdType.MESH
STRIP = 32
CHUNKS = 8


def dot_nn(a, b):
    return jnp.dot(a, b, preferred_element_type=jnp.float32)


def dot_tn(a, b):
    return lax.dot_general(a, b, (((0,), (0,)), ((), ())), preferred_element_type=jnp.float32)


def dot_nt(a, b):
    return lax.dot_general(a, b, (((1,), (1,)), ((), ())), preferred_element_type=jnp.float32)


def strips(rows, body, step=STRIP):
    def run(i, carry):
        body(pl.ds(pl.multiple_of(i * step, step), step))
        return carry

    lax.fori_loop(0, rows // step, run, 0)


def kernel(
    n_feat, n_grp, fine,
    src_hbm, cnt_hbm, feat_hbm, adj_hbm, ws_hbm, wn_hbm, mult_hbm, shift_hbm, cot_hbm,
    out_hbm, gfeat_hbm, grads_hbm,
    src_ref, cnt_ref, out_ref, gfeat_ref,
    adj_ref, ws_ref, wn_ref, mult_ref, shift_ref, cot_ref,
    pool, dense, dsum, inv, summed, preact, both, gpre,
    buf1, in2, buf2, in3, full,
    back, term_out, term_sum, own_grad, term_in,
    load_s, store_s, halo_s, halo_r, term_s, term_r,
    pair_s, pair_r, rs2_s, rs2_r, rs3_s, rs3_r,
    ag1_s, ag1_r, ag2_s, ag2_r, ag3_s, ag3_r,
):
    n_chip = n_feat // 2
    square = n_chip == 4
    me = lax.axis_index("feat")
    grp = lax.axis_index("grp")
    core = lax.rem(me, 2)
    chip = me // 2
    odd = lax.rem(chip, 2)
    partner = me + 1 - 2 * core
    num_blocks, num_slots, block_len, _ = adj_ref.shape
    rows, width = feat_hbm.shape
    lanes = buf1.shape[1]
    ahead = lax.rem(me + 2, n_feat)
    behind = lax.rem(me + n_feat - 2, n_feat)
    chip_peers = [2 * lax.rem(chip + j, n_chip) + core for j in range(1, n_chip)]
    grp_peers = [lax.rem(grp + j, n_grp) for j in range(1, n_grp)]
    x_slot = 4 - 4 * odd
    y_slot = 4 * odd
    x_peer = 2 * (chip + 1 - 2 * odd) + core
    y_peer = 2 * lax.rem(chip + 2, n_chip) + core

    def to_feat(peer):
        return (grp, peer)

    def to_grp(peer):
        return (peer, me)

    sent = []

    def send(src, dst, ssem, rsem, device):
        copy = pltpu.make_async_remote_copy(
            src_ref=src, dst_ref=dst, send_sem=ssem, recv_sem=rsem, device_id=device, device_id_type=MESH
        )
        copy.start()
        sent.append(copy)

    def landed(dst, rsem):
        pltpu.make_async_remote_copy(
            src_ref=dst, dst_ref=dst, send_sem=rsem, recv_sem=rsem, device_id=to_feat(partner), device_id_type=MESH
        ).wait_recv()

    loads = [
        pltpu.make_async_copy(src, dst, load_s.at[i])
        for i, (src, dst) in enumerate(
            (
                (feat_hbm, both.at[0]), (adj_hbm, adj_ref), (ws_hbm, ws_ref), (wn_hbm, wn_ref),
                (mult_hbm, mult_ref), (shift_hbm, shift_ref), (cot_hbm, cot_ref),
                (src_hbm, src_ref), (cnt_hbm, cnt_ref),
            )
        )
    ]
    barrier = pltpu.get_barrier_semaphore()
    partners = [to_feat(partner)] + [to_feat(p) for p in chip_peers] + [to_grp(p) for p in grp_peers]
    for device in partners:
        pl.semaphore_signal(barrier, inc=1, device_id=device, device_id_type=MESH)
    for load in loads:
        load.start()
    loads[0].wait()
    pl.semaphore_wait(barrier, len(partners))

    near = 3 - 2 * core
    passed = 1 + 2 * core
    far = 4 - 4 * core
    other = 4 * core
    step = rows // CHUNKS
    chunks = [pl.ds(c * step, step) for c in range(CHUNKS)]
    if square:
        for c, at in enumerate(chunks):
            send(both.at[0, at], pool.at[y_slot, at], halo_s.at[0, c], halo_r.at[y_slot, c], to_feat(x_peer))
    else:
        for c, at in enumerate(chunks):
            send(both.at[0, at], pool.at[0, at], halo_s.at[0, c], halo_r.at[0, c], to_feat(ahead))
            send(both.at[0, at], pool.at[4, at], halo_s.at[1, c], halo_r.at[4, c], to_feat(behind))
    send(both.at[0], both.at[2], halo_s.at[2, 0], halo_r.at[SPAN, 0], to_feat(partner))

    dsum[...] = jnp.zeros_like(dsum)
    for load in (loads[1], loads[7], loads[8]):
        load.wait()

    def build(piece):
        owner = lax.rem(me + piece - SPAN + n_feat, n_feat)
        for b in range(num_blocks):
            dst_rows = slice(b * block_len, (b + 1) * block_len)
            for h in range(num_blocks):
                source = owner * num_blocks + h
                acc = jnp.zeros((block_len, block_len), jnp.float32)
                for k in range(num_slots):
                    hit = jnp.logical_and(src_ref[b, k] == source, cnt_ref[b] > k)
                    acc = acc + adj_ref[b, k].astype(jnp.float32) * jnp.where(hit, 1.0, 0.0)
                dsum[dst_rows, :] += acc
                dense[piece, dst_rows, h * block_len : (h + 1) * block_len] = acc.astype(jnp.bfloat16)

    def norms():
        inv[...] = jnp.broadcast_to(lax.rsqrt(jnp.sum(dsum[...], axis=1, keepdims=True)), inv.shape)

    def own_preact():
        loads[2].wait()
        preact[...] = dot_nn(both[0], ws_ref[...])

    def own_rows():
        summed[...] = dot_nn(dense[SPAN], both[0])

    def near_rows():
        landed(both.at[2], halo_r.at[SPAN, 0])
        summed[...] += dot_nn(dense[near], both[2])

    work = [functools.partial(build, piece) for piece in range(WIN)] + [norms, own_preact, own_rows, near_rows]
    work.pop(0)()
    for c, at in enumerate(chunks):
        work.pop(0)()
        landed(pool.at[x_slot, at], halo_r.at[x_slot, c])
        if square:
            send(pool.at[x_slot, at], pool.at[y_slot, at], halo_s.at[1, c], halo_r.at[y_slot, c], to_feat(y_peer))
    summed[...] += dot_nn(dense[x_slot], pool[x_slot])
    for c, at in enumerate(chunks):
        landed(pool.at[y_slot, at], halo_r.at[y_slot, c])
        send(pool.at[far, at], pool.at[near, at], halo_s.at[3, c], halo_r.at[near, c], to_feat(partner))
    summed[...] += dot_nn(dense[y_slot], pool[y_slot])
    for load in loads[3:7]:
        load.wait()
    for c, at in enumerate(chunks):
        landed(pool.at[passed, at], halo_r.at[passed, c])
    summed[...] += dot_nn(dense[passed], pool[passed])

    def aggregate(at):
        both[1, at, :] = (summed[at, :] * inv[at, :1]).astype(jnp.bfloat16)

    strips(rows, aggregate)
    send(both.at[1], both.at[3], pair_s.at[0], pair_r.at[0], to_feat(partner))
    preact[...] += dot_nn(both[1], wn_ref[...])
    mult_ref[...] = mult_ref[...] * jnp.exp2(-shift_ref[...].astype(jnp.float32))

    tstep = rows // 2
    halves = [pl.ds(c * tstep, tstep) for c in range(2)]
    quarters = [pl.ds(c * (rows // 4), rows // 4) for c in range(4)]

    def activate(at):
        scale = mult_ref[...]
        scaled = preact[at, :] * scale
        gate = 1.0 / (1.0 + jnp.exp(-scaled))
        out_ref[at, :] = (scaled * gate).astype(jnp.bfloat16)
        gpre[0, at, :] = (
            cot_ref[at, :].astype(jnp.float32) * gate * (1.0 + scaled * (1.0 - gate)) * scale
        ).astype(jnp.bfloat16)

    for c, at in enumerate(halves):
        strips(tstep, lambda part, c=c: activate(pl.ds(c * tstep + part.start, part.size)))
        send(gpre.at[0, at], gpre.at[1, at], pair_s.at[1 + c], pair_r.at[1 + c], to_feat(partner))
    stores = []

    def store(src, dst):
        copy = pltpu.make_async_copy(src, dst, store_s.at[len(stores)])
        copy.start()
        stores.append(copy)

    store(out_ref, out_hbm)

    pulled = dot_nt(gpre[0], wn_ref[...])
    back[...] = (pulled * inv[:, :1]).astype(jnp.bfloat16)
    term_out[passed] = dot_tn(dense[passed], back[...]).astype(jnp.bfloat16)
    send(term_out.at[passed], term_in.at[2], term_s.at[0, 0], term_r.at[2, 0], to_feat(partner))

    half = buf1.shape[0]
    c2 = buf2.shape[0]
    c3 = c2 // n_grp
    order = [lax.rem(chip + j, n_chip) for j in range(1, n_chip + 1)]
    if fine:
        owners = [lax.rem(grp + 1 + q, n_grp) for q in range(n_grp)]
        cuts = [(pl.multiple_of(o * c3, c3), c3) for o in owners]
    else:
        cuts = [(0, c2)]

    def share_out(j):
        for q, (first, size) in enumerate(cuts):
            src = buf1.at[pl.ds(pl.multiple_of(order[j] * c2 + first, 16), size)]
            send(src, in2.at[j, pl.ds(first, size)], rs2_s.at[j, q], rs2_r.at[j, q], to_feat(chip_peers[j]))

    landed(both.at[3], pair_r.at[0])
    for c, at in enumerate(halves):
        landed(gpre.at[1, at], pair_r.at[1 + c])
    if lanes == gpre.shape[2]:
        for j in range(n_chip):
            at = pl.ds(pl.multiple_of(order[j] * c2, c2), c2)
            part = dot_tn(both[core, :, at], gpre[0]) + dot_tn(both[2 + core, :, at], gpre[1])
            buf1[at, :] = part.astype(jnp.bfloat16)
            if j < n_chip - 1:
                share_out(j)
    else:
        part = dot_tn(both[core], gpre[0]) + dot_tn(both[2 + core], gpre[1])
        for j in range(gpre.shape[2] // lanes):
            buf1[j * width : (j + 1) * width, :] = part[:, j * lanes : (j + 1) * lanes].astype(jnp.bfloat16)
        for j in range(n_chip - 1):
            share_out(j)

    term_sum[0] = dot_tn(dense[x_slot], back[...])
    term_sum[1] = dot_tn(dense[y_slot], back[...])
    landed(term_in.at[2], term_r.at[2, 0])
    through = lax.rem(core + chip, 2)
    term_sum[through] += term_in[2].astype(jnp.float32)
    for c, at in enumerate(quarters):
        term_out[y_slot, at, :] = term_sum[1, at, :].astype(jnp.bfloat16)
        if square:
            send(term_out.at[y_slot, at], term_in.at[1, at], term_s.at[1, c], term_r.at[1, c], to_feat(y_peer))
        else:
            target = lax.rem(me + y_slot - 2 + n_feat, n_feat)
            send(term_out.at[y_slot, at], term_in.at[odd, at], term_s.at[1, c], term_r.at[odd, c], to_feat(target))
    term_out[near] = dot_tn(dense[near], back[...]).astype(jnp.bfloat16)
    send(term_out.at[near], term_in.at[3], term_s.at[3, 0], term_r.at[3, 0], to_feat(partner))
    own_grad[...] = dot_nt(gpre[0], ws_ref[...])
    own_grad[...] += dot_tn(dense[SPAN], back[...])

    def send_terms():
        for c, at in enumerate(quarters):
            value = term_sum[0, at, :]
            if square:
                landed(term_in.at[1, at], term_r.at[1, c])
                value = value + term_in[1, at, :].astype(jnp.float32)
            term_out[x_slot, at, :] = value.astype(jnp.bfloat16)
            if square:
                send(term_out.at[x_slot, at], term_in.at[0, at], term_s.at[2, c], term_r.at[0, c], to_feat(x_peer))
            else:
                target = lax.rem(me + x_slot - 2 + n_feat, n_feat)
                place = 1 - odd
                send(term_out.at[x_slot, at], term_in.at[place, at], term_s.at[2, c], term_r.at[place, c], to_feat(target))

    if not fine:
        send_terms()

    for q, (first, size) in enumerate(cuts):
        at = pl.ds(first, size)
        total = buf1[pl.ds(pl.multiple_of(chip * c2 + first, 16), size), :].astype(jnp.float32)
        for j in range(n_chip - 1):
            landed(in2.at[j, at], rs2_r.at[j, q])
            total = total + in2[j, at, :].astype(jnp.float32)
        buf2[at, :] = total.astype(jnp.bfloat16)
        if fine and q < n_grp - 1:
            send(buf2.at[at], in3.at[q], rs3_s.at[q], rs3_r.at[q], to_grp(grp_peers[q]))
    if fine:
        send_terms()
    else:
        for j, peer in enumerate(grp_peers):
            at = pl.ds(pl.multiple_of(peer * c3, c3), c3)
            send(buf2.at[at], in3.at[j], rs3_s.at[j], rs3_r.at[j], to_grp(peer))
    total = buf2[pl.ds(pl.multiple_of(grp * c3, c3), c3), :].astype(jnp.float32)
    for j in range(n_grp - 1):
        landed(in3.at[j], rs3_r.at[j])
        total = total + in3[j].astype(jnp.float32)

    def piece3(owner):
        return full.at[pl.ds(pl.multiple_of(core * half + chip * c2 + owner * c3, c3), c3)]

    def piece2(side, owner):
        return full.at[pl.ds(pl.multiple_of(side * half + owner * c2, c2), c2)]

    def spread_piece(owner, q):
        for j, peer in enumerate((x_peer, y_peer) if square else chip_peers):
            send(piece3(owner), piece3(owner), ag2_s.at[j, q], ag2_r.at[j, q], to_feat(peer))

    piece3(grp)[...] = total.astype(jnp.bfloat16)
    for j, peer in enumerate(grp_peers):
        send(piece3(grp), piece3(grp), ag3_s.at[j], ag3_r.at[j], to_grp(peer))
    if fine:
        spread_piece(grp, 0)
    for j in range(n_grp - 1):
        owner = lax.rem(grp + n_grp - 1 - j, n_grp)
        landed(piece3(owner), ag3_r.at[j])
        if fine:
            spread_piece(owner, j + 1)
    if not fine:
        for j, peer in enumerate(chip_peers):
            send(piece2(core, chip), piece2(core, chip), ag2_s.at[j, 0], ag2_r.at[j, 0], to_feat(peer))
    send(piece2(core, chip), piece2(core, chip), ag1_s.at[0], ag1_r.at[0], to_feat(partner))

    def piece_of(owner, q):
        if not fine:
            return piece2(core, owner)
        first = core * half + owner * c2 + lax.rem(grp + n_grp - q, n_grp) * c3
        return full.at[pl.ds(pl.multiple_of(first, c3), c3)]

    if square:
        sources = [x_peer // 2, y_peer // 2, lax.rem(x_peer // 2 + 2, n_chip)]
        for q in range(len(cuts)):
            for j in range(2):
                landed(piece_of(sources[j], q), ag2_r.at[j, q])
                if j == q % 2:
                    piece = piece_of(sources[j], q)
                    send(piece, piece, ag2_s.at[2, q], ag2_r.at[2, q], to_feat((y_peer, x_peer)[j]))
        for j in range(2):
            place = piece2(core, sources[j])
            send(place, place, ag1_s.at[j + 1], ag1_r.at[j + 1], to_feat(partner))
    else:
        sources = [lax.rem(chip + n_chip - 1 - j, n_chip) for j in range(n_chip - 1)]

    arrivals = (0, 3) if square else (0, 1, 3)
    for slot in arrivals:
        if slot == 3:
            landed(term_in.at[3], term_r.at[3, 0])
        else:
            for c, at in enumerate(quarters):
                landed(term_in.at[slot, at], term_r.at[slot, c])

    def finish(at):
        grad = own_grad[at, :]
        for slot in arrivals:
            grad = grad + term_in[slot, at, :].astype(jnp.float32)
        gfeat_ref[at, :] = grad.astype(jnp.bfloat16)

    strips(rows, finish)
    store(gfeat_ref, gfeat_hbm)

    for j in range(2 if square else 0, n_chip - 1):
        for q in range(len(cuts)):
            landed(piece_of(sources[j], q), ag2_r.at[j, q])
        place = piece2(core, sources[j])
        send(place, place, ag1_s.at[j + 1], ag1_r.at[j + 1], to_feat(partner))
    own_half = pl.ds(pl.multiple_of(core * half, half), half)
    store(full.at[own_half], grads_hbm.at[own_half])
    for j, owner in enumerate([chip] + sources):
        landed(piece2(1 - core, owner), ag1_r.at[j])
    its_half = pl.ds(pl.multiple_of((1 - core) * half, half), half)
    store(full.at[its_half], grads_hbm.at[its_half])
    for copy in sent:
        copy.wait_send()
    for copy in stores:
        copy.wait()


def place_outputs(
    grad_scale, out_in, gfeat_in, grads_in, out_hbm, gfeat_hbm, self_hbm, neigh_hbm,
    held, scaled, out_held, gfeat_held, load_s, store_s
):
    part = held.shape[1]
    loads = [
        pltpu.make_async_copy(grads_in.at[pl.ds(i * part, part)], held.at[i], load_s.at[i]) for i in range(4)
    ]
    fetches = [
        pltpu.make_async_copy(out_in, out_held, load_s.at[4]),
        pltpu.make_async_copy(gfeat_in, gfeat_held, load_s.at[5]),
    ]
    for copy in loads + fetches:
        copy.start()
    moves = []
    for i in range(4):
        loads[i].wait()

        def widen(at, i=i):
            scaled[i, at, :] = held[i, at, :].astype(jnp.float32) * grad_scale

        strips(part, widen, 64)
        dst = (self_hbm, neigh_hbm)[i // 2].at[pl.ds((i % 2) * part, part)]
        store = pltpu.make_async_copy(scaled.at[i], dst, store_s.at[i])
        store.start()
        moves.append(store)
    for i, (src, dst) in enumerate(((out_held, out_hbm), (gfeat_held, gfeat_hbm))):
        fetches[i].wait()
        move = pltpu.make_async_copy(src, dst, store_s.at[4 + i])
        move.start()
        moves.append(move)
    for copy in moves:
        copy.wait()


def local(
    n_feat, n_grp, features, adj_tiles, src_block, counts, w_self, w_neigh, multiplier, bit_shift, cotangent
):
    rows, width = features.shape
    hidden = w_self.shape[1]
    n_chip = n_feat // 2
    lanes = hidden if width % (16 * n_chip * n_grp) == 0 else 128
    fine = n_chip * n_grp <= 16
    half = width * hidden // lanes
    c2 = half // n_chip
    c3 = c2 // n_grp
    bf, f32 = jnp.bfloat16, jnp.float32
    hbm = pl.BlockSpec(memory_space=pltpu.HBM)
    dma = pltpu.SemaphoreType.DMA
    cuts = n_grp if fine else 1
    output, grad_features, grads = pl.pallas_call(
        functools.partial(kernel, n_feat, n_grp, fine),
        out_shape=(
            jax.ShapeDtypeStruct((rows, hidden), bf),
            jax.ShapeDtypeStruct((rows, width), bf),
            jax.ShapeDtypeStruct((2 * half, lanes), bf),
        ),
        in_specs=[hbm] * 9,
        out_specs=(hbm, hbm, hbm),
        scratch_shapes=[
            pltpu.SMEM(src_block.shape, jnp.int32),
            pltpu.SMEM(counts.shape, jnp.int32),
            pltpu.VMEM((rows, hidden), bf),
            pltpu.VMEM((rows, width), bf),
            pltpu.VMEM(adj_tiles.shape, bf),
            pltpu.VMEM(w_self.shape, bf),
            pltpu.VMEM(w_neigh.shape, bf),
            pltpu.VMEM((1, hidden), f32),
            pltpu.VMEM((1, hidden), jnp.int32),
            pltpu.VMEM((rows, hidden), bf),
            pltpu.VMEM((WIN, rows, width), bf),
            pltpu.VMEM((WIN, rows, rows), bf),
            pltpu.VMEM((rows, adj_tiles.shape[3]), f32),
            pltpu.VMEM((rows, 128), f32),
            pltpu.VMEM((rows, width), f32),
            pltpu.VMEM((rows, hidden), f32),
            pltpu.VMEM((4, rows, width), bf),
            pltpu.VMEM((2, rows, hidden), bf),
            pltpu.VMEM((half, lanes), bf),
            pltpu.VMEM((n_chip - 1, c2, lanes), bf),
            pltpu.VMEM((c2, lanes), bf),
            pltpu.VMEM((n_grp - 1, c3, lanes), bf),
            pltpu.VMEM((2 * half, lanes), bf),
            pltpu.VMEM((rows, width), bf),
            pltpu.VMEM((WIN, rows, width), bf),
            pltpu.VMEM((2, rows, width), f32),
            pltpu.VMEM((rows, width), f32),
            pltpu.VMEM((4, rows, width), bf),
            dma((9,)), dma((4,)), dma((4, CHUNKS)), dma((WIN, CHUNKS)), dma((4, 4)), dma((4, 4)),
            dma((3,)), dma((3,)), dma((n_chip - 1, cuts)), dma((n_chip - 1, cuts)),
            dma((n_grp - 1,)), dma((n_grp - 1,)),
            dma((n_chip,)), dma((n_chip,)), dma((n_chip - 1, cuts)), dma((n_chip - 1, cuts)),
            dma((n_grp - 1,)), dma((n_grp - 1,)),
        ],
        compiler_params=pltpu.CompilerParams(
            collective_id=0, has_side_effects=True, vmem_limit_bytes=62 * 1024 * 1024
        ),
    )(
        src_block, counts, features, adj_tiles, w_self, w_neigh,
        multiplier.reshape(1, hidden), bit_shift.reshape(1, hidden), cotangent,
    )
    grad_scale = 1.0 / math.sqrt(rows * n_grp * n_feat)
    if lanes != hidden:
        grads = grads.reshape(2, hidden // lanes, width, lanes).transpose(0, 2, 1, 3).reshape(2 * width, hidden)
    return pl.pallas_call(
        functools.partial(place_outputs, grad_scale),
        out_shape=(
            jax.ShapeDtypeStruct(output.shape, bf),
            jax.ShapeDtypeStruct(grad_features.shape, bf),
            jax.ShapeDtypeStruct((width, hidden), f32),
            jax.ShapeDtypeStruct((width, hidden), f32),
        ),
        in_specs=[hbm] * 3,
        out_specs=(hbm,) * 4,
        scratch_shapes=[
            pltpu.VMEM((4, width // 2, hidden), bf),
            pltpu.VMEM((4, width // 2, hidden), f32),
            pltpu.VMEM(output.shape, bf),
            pltpu.VMEM(grad_features.shape, bf),
            dma((6,)),
            dma((6,)),
        ],
        compiler_params=pltpu.CompilerParams(vmem_limit_bytes=62 * 1024 * 1024),
    )(output, grad_features, grads)


def solution(mesh):
    return jax.shard_map(
        functools.partial(local, mesh.shape["feat"], mesh.shape["grp"]),
        mesh=mesh,
        in_specs=(
            P(("grp", "feat"), None),
            P(("grp", "feat"), None, None, None),
            P(("grp", "feat"), None),
            P(("grp", "feat")),
            P(),
            P(),
            P(),
            P(),
            P(("grp", "feat"), None),
        ),
        out_specs=(P(("grp", "feat"), None), P(("grp", "feat"), None), P(), P()),
        check_vma=False,
    )
```

```python
import functools
import math

import jax
import jax.numpy as jnp
from jax import lax
from jax.experimental import pallas as pl
from jax.experimental.pallas import tpu as pltpu
from jax.sharding import PartitionSpec as P

SPAN = 2
WIN = 2 * SPAN + 1
MESH = pl.DeviceIdType.MESH
STRIP = 32
CHUNKS = 8


def dot_nn(a, b):
    return jnp.dot(a, b, preferred_element_type=jnp.float32)


def dot_tn(a, b):
    return lax.dot_general(a, b, (((0,), (0,)), ((), ())), preferred_element_type=jnp.float32)


def dot_nt(a, b):
    return lax.dot_general(a, b, (((1,), (1,)), ((), ())), preferred_element_type=jnp.float32)


def strips(rows, body, step=STRIP):
    def run(i, carry):
        body(pl.ds(pl.multiple_of(i * step, step), step))
        return carry

    lax.fori_loop(0, rows // step, run, 0)


def kernel(
    n_feat, n_grp, fine,
    src_hbm, cnt_hbm, feat_hbm, adj_hbm, ws_hbm, wn_hbm, mult_hbm, shift_hbm, cot_hbm,
    out_hbm, gfeat_hbm, grads_hbm,
    src_ref, cnt_ref, out_ref, gfeat_ref,
    adj_ref, ws_ref, wn_ref, mult_ref, shift_ref, cot_ref,
    pool, dense, dsum, inv, summed, preact, both, gpre,
    buf1, in2, buf2, in3, full,
    back, term_out, term_sum, own_grad, term_in,
    load_s, store_s, halo_s, halo_r, term_s, term_r,
    pair_s, pair_r, rs2_s, rs2_r, rs3_s, rs3_r,
    ag1_s, ag1_r, ag2_s, ag2_r, ag3_s, ag3_r,
):
    n_chip = n_feat // 2
    square = n_chip == 4
    me = lax.axis_index("feat")
    grp = lax.axis_index("grp")
    core = lax.rem(me, 2)
    chip = me // 2
    odd = lax.rem(chip, 2)
    partner = me + 1 - 2 * core
    num_blocks, num_slots, block_len, _ = adj_ref.shape
    rows, width = feat_hbm.shape
    lanes = buf1.shape[1]
    ahead = lax.rem(me + 2, n_feat)
    behind = lax.rem(me + n_feat - 2, n_feat)
    chip_peers = [2 * lax.rem(chip + j, n_chip) + core for j in range(1, n_chip)]
    grp_peers = [lax.rem(grp + j, n_grp) for j in range(1, n_grp)]
    x_slot = 4 - 4 * odd
    y_slot = 4 * odd
    x_peer = 2 * (chip + 1 - 2 * odd) + core
    y_peer = 2 * lax.rem(chip + 2, n_chip) + core

    def to_feat(peer):
        return (grp, peer)

    def to_grp(peer):
        return (peer, me)

    sent = []

    def send(src, dst, ssem, rsem, device):
        copy = pltpu.make_async_remote_copy(
            src_ref=src, dst_ref=dst, send_sem=ssem, recv_sem=rsem, device_id=device, device_id_type=MESH
        )
        copy.start()
        sent.append(copy)

    def landed(dst, rsem):
        pltpu.make_async_remote_copy(
            src_ref=dst, dst_ref=dst, send_sem=rsem, recv_sem=rsem, device_id=to_feat(partner), device_id_type=MESH
        ).wait_recv()

    loads = [
        pltpu.make_async_copy(src, dst, load_s.at[i])
        for i, (src, dst) in enumerate(
            (
                (feat_hbm, both.at[0]), (adj_hbm, adj_ref), (ws_hbm, ws_ref), (wn_hbm, wn_ref),
                (mult_hbm, mult_ref), (shift_hbm, shift_ref), (cot_hbm, cot_ref),
                (src_hbm, src_ref), (cnt_hbm, cnt_ref),
            )
        )
    ]
    barrier = pltpu.get_barrier_semaphore()
    partners = [to_feat(partner)] + [to_feat(p) for p in chip_peers] + [to_grp(p) for p in grp_peers]
    for device in partners:
        pl.semaphore_signal(barrier, inc=1, device_id=device, device_id_type=MESH)
    for load in loads:
        load.start()
    loads[0].wait()
    pl.semaphore_wait(barrier, len(partners))

    near = 3 - 2 * core
    passed = 1 + 2 * core
    far = 4 - 4 * core
    other = 4 * core
    step = rows // CHUNKS
    chunks = [pl.ds(c * step, step) for c in range(CHUNKS)]
    if square:
        for c, at in enumerate(chunks):
            send(both.at[0, at], pool.at[y_slot, at], halo_s.at[0, c], halo_r.at[y_slot, c], to_feat(x_peer))
    else:
        for c, at in enumerate(chunks):
            send(both.at[0, at], pool.at[0, at], halo_s.at[0, c], halo_r.at[0, c], to_feat(ahead))
            send(both.at[0, at], pool.at[4, at], halo_s.at[1, c], halo_r.at[4, c], to_feat(behind))
    send(both.at[0], both.at[2], halo_s.at[2, 0], halo_r.at[SPAN, 0], to_feat(partner))

    dsum[...] = jnp.zeros_like(dsum)
    for load in (loads[1], loads[7], loads[8]):
        load.wait()

    def build(piece):
        owner = lax.rem(me + piece - SPAN + n_feat, n_feat)
        for b in range(num_blocks):
            dst_rows = slice(b * block_len, (b + 1) * block_len)
            for h in range(num_blocks):
                source = owner * num_blocks + h
                acc = jnp.zeros((block_len, block_len), jnp.float32)
                for k in range(num_slots):
                    hit = jnp.logical_and(src_ref[b, k] == source, cnt_ref[b] > k)
                    acc = acc + adj_ref[b, k].astype(jnp.float32) * jnp.where(hit, 1.0, 0.0)
                dsum[dst_rows, :] += acc
                dense[piece, dst_rows, h * block_len : (h + 1) * block_len] = acc.astype(jnp.bfloat16)

    def norms():
        inv[...] = jnp.broadcast_to(lax.rsqrt(jnp.sum(dsum[...], axis=1, keepdims=True)), inv.shape)

    def own_preact():
        loads[2].wait()
        preact[...] = dot_nn(both[0], ws_ref[...])

    def own_rows():
        summed[...] = dot_nn(dense[SPAN], both[0])

    def near_rows():
        landed(both.at[2], halo_r.at[SPAN, 0])
        summed[...] += dot_nn(dense[near], both[2])

    work = [functools.partial(build, piece) for piece in range(WIN)] + [norms, own_preact, own_rows, near_rows]
    work.pop(0)()
    for c, at in enumerate(chunks):
        work.pop(0)()
        landed(pool.at[x_slot, at], halo_r.at[x_slot, c])
        if square:
            send(pool.at[x_slot, at], pool.at[y_slot, at], halo_s.at[1, c], halo_r.at[y_slot, c], to_feat(y_peer))
    summed[...] += dot_nn(dense[x_slot], pool[x_slot])
    for c, at in enumerate(chunks):
        landed(pool.at[y_slot, at], halo_r.at[y_slot, c])
        send(pool.at[far, at], pool.at[near, at], halo_s.at[3, c], halo_r.at[near, c], to_feat(partner))
    summed[...] += dot_nn(dense[y_slot], pool[y_slot])
    for load in loads[3:7]:
        load.wait()
    for c, at in enumerate(chunks):
        landed(pool.at[passed, at], halo_r.at[passed, c])
    summed[...] += dot_nn(dense[passed], pool[passed])

    def aggregate(at):
        both[1, at, :] = (summed[at, :] * inv[at, :1]).astype(jnp.bfloat16)

    strips(rows, aggregate)
    send(both.at[1], both.at[3], pair_s.at[0], pair_r.at[0], to_feat(partner))
    preact[...] += dot_nn(both[1], wn_ref[...])
    mult_ref[...] = mult_ref[...] * jnp.exp2(-shift_ref[...].astype(jnp.float32))

    tstep = rows // 2
    halves = [pl.ds(c * tstep, tstep) for c in range(2)]
    quarters = [pl.ds(c * (rows // 4), rows // 4) for c in range(4)]

    def activate(at):
        scale = mult_ref[...]
        scaled = preact[at, :] * scale
        gate = 1.0 / (1.0 + jnp.exp(-scaled))
        out_ref[at, :] = (scaled * gate).astype(jnp.bfloat16)
        gpre[0, at, :] = (
            cot_ref[at, :].astype(jnp.float32) * gate * (1.0 + scaled * (1.0 - gate)) * scale
        ).astype(jnp.bfloat16)

    for c, at in enumerate(halves):
        strips(tstep, lambda part, c=c: activate(pl.ds(c * tstep + part.start, part.size)))
        send(gpre.at[0, at], gpre.at[1, at], pair_s.at[1 + c], pair_r.at[1 + c], to_feat(partner))
    stores = []

    def store(src, dst):
        copy = pltpu.make_async_copy(src, dst, store_s.at[len(stores)])
        copy.start()
        stores.append(copy)

    store(out_ref, out_hbm)

    pulled = dot_nt(gpre[0], wn_ref[...])
    back[...] = (pulled * inv[:, :1]).astype(jnp.bfloat16)
    term_out[passed] = dot_tn(dense[passed], back[...]).astype(jnp.bfloat16)
    send(term_out.at[passed], term_in.at[2], term_s.at[0, 0], term_r.at[2, 0], to_feat(partner))

    half = buf1.shape[0]
    c2 = buf2.shape[0]
    c3 = c2 // n_grp
    order = [lax.rem(chip + j, n_chip) for j in range(1, n_chip + 1)]
    if fine:
        owners = [lax.rem(grp + 1 + q, n_grp) for q in range(n_grp)]
        cuts = [(pl.multiple_of(o * c3, c3), c3) for o in owners]
    else:
        cuts = [(0, c2)]

    def share_out(j):
        for q, (first, size) in enumerate(cuts):
            src = buf1.at[pl.ds(pl.multiple_of(order[j] * c2 + first, 16), size)]
            send(src, in2.at[j, pl.ds(first, size)], rs2_s.at[j, q], rs2_r.at[j, q], to_feat(chip_peers[j]))

    landed(both.at[3], pair_r.at[0])
    for c, at in enumerate(halves):
        landed(gpre.at[1, at], pair_r.at[1 + c])
    if lanes == gpre.shape[2]:
        for j in range(n_chip):
            at = pl.ds(pl.multiple_of(order[j] * c2, c2), c2)
            part = dot_tn(both[core, :, at], gpre[0]) + dot_tn(both[2 + core, :, at], gpre[1])
            buf1[at, :] = part.astype(jnp.bfloat16)
            if j < n_chip - 1:
                share_out(j)
    else:
        part = dot_tn(both[core], gpre[0]) + dot_tn(both[2 + core], gpre[1])
        for j in range(gpre.shape[2] // lanes):
            buf1[j * width : (j + 1) * width, :] = part[:, j * lanes : (j + 1) * lanes].astype(jnp.bfloat16)
        for j in range(n_chip - 1):
            share_out(j)

    term_sum[0] = dot_tn(dense[x_slot], back[...])
    term_sum[1] = dot_tn(dense[y_slot], back[...])
    landed(term_in.at[2], term_r.at[2, 0])
    through = lax.rem(core + chip, 2)
    term_sum[through] += term_in[2].astype(jnp.float32)
    for c, at in enumerate(quarters):
        term_out[y_slot, at, :] = term_sum[1, at, :].astype(jnp.bfloat16)
        if square:
            send(term_out.at[y_slot, at], term_in.at[1, at], term_s.at[1, c], term_r.at[1, c], to_feat(y_peer))
        else:
            target = lax.rem(me + y_slot - 2 + n_feat, n_feat)
            send(term_out.at[y_slot, at], term_in.at[odd, at], term_s.at[1, c], term_r.at[odd, c], to_feat(target))
    term_out[near] = dot_tn(dense[near], back[...]).astype(jnp.bfloat16)
    send(term_out.at[near], term_in.at[3], term_s.at[3, 0], term_r.at[3, 0], to_feat(partner))
    own_grad[...] = dot_nt(gpre[0], ws_ref[...])
    own_grad[...] += dot_tn(dense[SPAN], back[...])

    def send_terms():
        for c, at in enumerate(quarters):
            value = term_sum[0, at, :]
            if square:
                landed(term_in.at[1, at], term_r.at[1, c])
                value = value + term_in[1, at, :].astype(jnp.float32)
            term_out[x_slot, at, :] = value.astype(jnp.bfloat16)
            if square:
                send(term_out.at[x_slot, at], term_in.at[0, at], term_s.at[2, c], term_r.at[0, c], to_feat(x_peer))
            else:
                target = lax.rem(me + x_slot - 2 + n_feat, n_feat)
                place = 1 - odd
                send(term_out.at[x_slot, at], term_in.at[place, at], term_s.at[2, c], term_r.at[place, c], to_feat(target))

    send_terms()

    for q, (first, size) in enumerate(cuts):
        at = pl.ds(first, size)
        total = buf1[pl.ds(pl.multiple_of(chip * c2 + first, 16), size), :].astype(jnp.float32)
        for j in range(n_chip - 1):
            landed(in2.at[j, at], rs2_r.at[j, q])
            total = total + in2[j, at, :].astype(jnp.float32)
        buf2[at, :] = total.astype(jnp.bfloat16)
        if fine and q < n_grp - 1:
            send(buf2.at[at], in3.at[q], rs3_s.at[q], rs3_r.at[q], to_grp(grp_peers[q]))
    if not fine:
        for j, peer in enumerate(grp_peers):
            at = pl.ds(pl.multiple_of(peer * c3, c3), c3)
            send(buf2.at[at], in3.at[j], rs3_s.at[j], rs3_r.at[j], to_grp(peer))
    total = buf2[pl.ds(pl.multiple_of(grp * c3, c3), c3), :].astype(jnp.float32)
    for j in range(n_grp - 1):
        landed(in3.at[j], rs3_r.at[j])
        total = total + in3[j].astype(jnp.float32)

    def piece3(owner):
        return full.at[pl.ds(pl.multiple_of(core * half + chip * c2 + owner * c3, c3), c3)]

    def piece2(side, owner):
        return full.at[pl.ds(pl.multiple_of(side * half + owner * c2, c2), c2)]

    def spread_piece(owner, q):
        for j, peer in enumerate((x_peer, y_peer) if square else chip_peers):
            send(piece3(owner), piece3(owner), ag2_s.at[j, q], ag2_r.at[j, q], to_feat(peer))

    piece3(grp)[...] = total.astype(jnp.bfloat16)
    for j, peer in enumerate(grp_peers):
        send(piece3(grp), piece3(grp), ag3_s.at[j], ag3_r.at[j], to_grp(peer))
    if fine:
        spread_piece(grp, 0)
    for j in range(n_grp - 1):
        owner = lax.rem(grp + n_grp - 1 - j, n_grp)
        landed(piece3(owner), ag3_r.at[j])
        if fine:
            spread_piece(owner, j + 1)
    if not fine:
        for j, peer in enumerate(chip_peers):
            send(piece2(core, chip), piece2(core, chip), ag2_s.at[j, 0], ag2_r.at[j, 0], to_feat(peer))
    send(piece2(core, chip), piece2(core, chip), ag1_s.at[0], ag1_r.at[0], to_feat(partner))

    def piece_of(owner, q):
        if not fine:
            return piece2(core, owner)
        first = core * half + owner * c2 + lax.rem(grp + n_grp - q, n_grp) * c3
        return full.at[pl.ds(pl.multiple_of(first, c3), c3)]

    if square:
        sources = [x_peer // 2, y_peer // 2, lax.rem(x_peer // 2 + 2, n_chip)]
        for q in range(len(cuts)):
            for j in range(2):
                landed(piece_of(sources[j], q), ag2_r.at[j, q])
                if j == q % 2:
                    piece = piece_of(sources[j], q)
                    send(piece, piece, ag2_s.at[2, q], ag2_r.at[2, q], to_feat((y_peer, x_peer)[j]))
        for j in range(2):
            place = piece2(core, sources[j])
            send(place, place, ag1_s.at[j + 1], ag1_r.at[j + 1], to_feat(partner))
    else:
        sources = [lax.rem(chip + n_chip - 1 - j, n_chip) for j in range(n_chip - 1)]

    arrivals = (0, 3) if square else (0, 1, 3)
    for slot in arrivals:
        if slot == 3:
            landed(term_in.at[3], term_r.at[3, 0])
        else:
            for c, at in enumerate(quarters):
                landed(term_in.at[slot, at], term_r.at[slot, c])

    def finish(at):
        grad = own_grad[at, :]
        for slot in arrivals:
            grad = grad + term_in[slot, at, :].astype(jnp.float32)
        gfeat_ref[at, :] = grad.astype(jnp.bfloat16)

    strips(rows, finish)
    store(gfeat_ref, gfeat_hbm)

    for j in range(2 if square else 0, n_chip - 1):
        for q in range(len(cuts)):
            landed(piece_of(sources[j], q), ag2_r.at[j, q])
        place = piece2(core, sources[j])
        send(place, place, ag1_s.at[j + 1], ag1_r.at[j + 1], to_feat(partner))
    own_half = pl.ds(pl.multiple_of(core * half, half), half)
    store(full.at[own_half], grads_hbm.at[own_half])
    for j, owner in enumerate([chip] + sources):
        landed(piece2(1 - core, owner), ag1_r.at[j])
    its_half = pl.ds(pl.multiple_of((1 - core) * half, half), half)
    store(full.at[its_half], grads_hbm.at[its_half])
    for copy in sent:
        copy.wait_send()
    for copy in stores:
        copy.wait()


def place_outputs(
    grad_scale, out_in, gfeat_in, grads_in, out_hbm, gfeat_hbm, self_hbm, neigh_hbm,
    held, scaled, out_held, gfeat_held, load_s, store_s
):
    part = held.shape[1]
    loads = [
        pltpu.make_async_copy(grads_in.at[pl.ds(i * part, part)], held.at[i], load_s.at[i]) for i in range(4)
    ]
    fetches = [
        pltpu.make_async_copy(out_in, out_held, load_s.at[4]),
        pltpu.make_async_copy(gfeat_in, gfeat_held, load_s.at[5]),
    ]
    for copy in loads + fetches:
        copy.start()
    moves = []
    for i in range(4):
        loads[i].wait()

        def widen(at, i=i):
            scaled[i, at, :] = held[i, at, :].astype(jnp.float32) * grad_scale

        strips(part, widen, 64)
        dst = (self_hbm, neigh_hbm)[i // 2].at[pl.ds((i % 2) * part, part)]
        store = pltpu.make_async_copy(scaled.at[i], dst, store_s.at[i])
        store.start()
        moves.append(store)
    for i, (src, dst) in enumerate(((out_held, out_hbm), (gfeat_held, gfeat_hbm))):
        fetches[i].wait()
        move = pltpu.make_async_copy(src, dst, store_s.at[4 + i])
        move.start()
        moves.append(move)
    for copy in moves:
        copy.wait()


def local(
    n_feat, n_grp, features, adj_tiles, src_block, counts, w_self, w_neigh, multiplier, bit_shift, cotangent
):
    rows, width = features.shape
    hidden = w_self.shape[1]
    n_chip = n_feat // 2
    lanes = hidden if width % (16 * n_chip * n_grp) == 0 else 128
    fine = n_chip * n_grp <= 16
    half = width * hidden // lanes
    c2 = half // n_chip
    c3 = c2 // n_grp
    bf, f32 = jnp.bfloat16, jnp.float32
    hbm = pl.BlockSpec(memory_space=pltpu.HBM)
    dma = pltpu.SemaphoreType.DMA
    cuts = n_grp if fine else 1
    output, grad_features, grads = pl.pallas_call(
        functools.partial(kernel, n_feat, n_grp, fine),
        out_shape=(
            jax.ShapeDtypeStruct((rows, hidden), bf),
            jax.ShapeDtypeStruct((rows, width), bf),
            jax.ShapeDtypeStruct((2 * half, lanes), bf),
        ),
        in_specs=[hbm] * 9,
        out_specs=(hbm, hbm, hbm),
        scratch_shapes=[
            pltpu.SMEM(src_block.shape, jnp.int32),
            pltpu.SMEM(counts.shape, jnp.int32),
            pltpu.VMEM((rows, hidden), bf),
            pltpu.VMEM((rows, width), bf),
            pltpu.VMEM(adj_tiles.shape, bf),
            pltpu.VMEM(w_self.shape, bf),
            pltpu.VMEM(w_neigh.shape, bf),
            pltpu.VMEM((1, hidden), f32),
            pltpu.VMEM((1, hidden), jnp.int32),
            pltpu.VMEM((rows, hidden), bf),
            pltpu.VMEM((WIN, rows, width), bf),
            pltpu.VMEM((WIN, rows, rows), bf),
            pltpu.VMEM((rows, adj_tiles.shape[3]), f32),
            pltpu.VMEM((rows, 128), f32),
            pltpu.VMEM((rows, width), f32),
            pltpu.VMEM((rows, hidden), f32),
            pltpu.VMEM((4, rows, width), bf),
            pltpu.VMEM((2, rows, hidden), bf),
            pltpu.VMEM((half, lanes), bf),
            pltpu.VMEM((n_chip - 1, c2, lanes), bf),
            pltpu.VMEM((c2, lanes), bf),
            pltpu.VMEM((n_grp - 1, c3, lanes), bf),
            pltpu.VMEM((2 * half, lanes), bf),
            pltpu.VMEM((rows, width), bf),
            pltpu.VMEM((WIN, rows, width), bf),
            pltpu.VMEM((2, rows, width), f32),
            pltpu.VMEM((rows, width), f32),
            pltpu.VMEM((4, rows, width), bf),
            dma((9,)), dma((4,)), dma((4, CHUNKS)), dma((WIN, CHUNKS)), dma((4, 4)), dma((4, 4)),
            dma((3,)), dma((3,)), dma((n_chip - 1, cuts)), dma((n_chip - 1, cuts)),
            dma((n_grp - 1,)), dma((n_grp - 1,)),
            dma((n_chip,)), dma((n_chip,)), dma((n_chip - 1, cuts)), dma((n_chip - 1, cuts)),
            dma((n_grp - 1,)), dma((n_grp - 1,)),
        ],
        compiler_params=pltpu.CompilerParams(
            collective_id=0, has_side_effects=True, vmem_limit_bytes=62 * 1024 * 1024
        ),
    )(
        src_block, counts, features, adj_tiles, w_self, w_neigh,
        multiplier.reshape(1, hidden), bit_shift.reshape(1, hidden), cotangent,
    )
    grad_scale = 1.0 / math.sqrt(rows * n_grp * n_feat)
    if lanes != hidden:
        grads = grads.reshape(2, hidden // lanes, width, lanes).transpose(0, 2, 1, 3).reshape(2 * width, hidden)
    return pl.pallas_call(
        functools.partial(place_outputs, grad_scale),
        out_shape=(
            jax.ShapeDtypeStruct(output.shape, bf),
            jax.ShapeDtypeStruct(grad_features.shape, bf),
            jax.ShapeDtypeStruct((width, hidden), f32),
            jax.ShapeDtypeStruct((width, hidden), f32),
        ),
        in_specs=[hbm] * 3,
        out_specs=(hbm,) * 4,
        scratch_shapes=[
            pltpu.VMEM((4, width // 2, hidden), bf),
            pltpu.VMEM((4, width // 2, hidden), f32),
            pltpu.VMEM(output.shape, bf),
            pltpu.VMEM(grad_features.shape, bf),
            dma((6,)),
            dma((6,)),
        ],
        compiler_params=pltpu.CompilerParams(vmem_limit_bytes=62 * 1024 * 1024),
    )(output, grad_features, grads)


def solution(mesh):
    return jax.shard_map(
        functools.partial(local, mesh.shape["feat"], mesh.shape["grp"]),
        mesh=mesh,
        in_specs=(
            P(("grp", "feat"), None),
            P(("grp", "feat"), None, None, None),
            P(("grp", "feat"), None),
            P(("grp", "feat")),
            P(),
            P(),
            P(),
            P(),
            P(("grp", "feat"), None),
        ),
        out_specs=(P(("grp", "feat"), None), P(("grp", "feat"), None), P(), P()),
        check_vma=False,
    )
```
